32 devices in a mesh: rad: 4 (over x, core), azi: 8 (over z, y).
Axes of the slice: x: 2, y: 2, z: 4, core: 2. Of those that a mesh axis runs over, the one named last changes fastest.
Arguments:
- fields: float32 [3, 8, 32, 1024], P(None, None, 'rad', 'azi'), may hold values from -6 to 6
- viscosity: float32 [32, 1024], P('rad', 'azi'), may hold values from 0.05 to 0.5
- rotation: float32 [32], replicated, may hold values from 0.2 to 2
- shift_blocks: int32 [1, 32], replicated, may hold values from 0 to 15
Outputs:
- fields_out: float32 [3, 8, 32, 1024], P(None, None, 'rad', 'azi')
The draws below stay inside these ranges and needn't reach their ends.
Inputs may be any that keep to these rules, and one draw needn't show every extreme that they name: `shift_blocks`: shift of radius r after step t, in blocks of 64 azimuth cells.
All inputs are finite; a program needn't handle non-finite values.
Results may differ from the reference program's by a relative error of at most 0.00002.
Values sent between devices are 32-bit elements; how exact they have to be, the bound alone decides.
A program may use at most 64 MiB of HBM per device.

```python
import math
import jax
import jax.numpy as jnp
from jax import lax

H = 8
BLOCK = 64
STEPS = 1
NR = 32
NA = 1024
NB = 16


def place_ends(values, stream_key, smallest, top_value):
    place = [jax.random.randint(jax.random.fold_in(stream_key, axis), (), 0, length) for axis, length in enumerate(values.shape)]
    main_axis = values.shape.index(max(values.shape))
    neighbour = place[:main_axis] + [(place[main_axis] + 1) % values.shape[main_axis]] + place[main_axis + 1:]
    return values.at[tuple(place)].set(smallest).at[tuple(neighbour)].set(top_value)


def steps_of(own_key, extent, pieces, least, largest):
    loudness = 1.0
    for position, parts in pieces:
        steps = jax.random.uniform(jax.random.fold_in(jax.random.fold_in(own_key, 6), position), (parts,), jnp.float32, least / len(pieces), largest / len(pieces))
        loudness = loudness * jnp.repeat(jnp.exp(steps), extent[position] // parts).reshape((-1,) + (1,) * (len(extent) - 1 - position))
    return loudness


def noise(stream_key, shape, scale, reach, shards=(), dtype=jnp.bfloat16):
    drawn = scale * jax.random.normal(stream_key, shape, jnp.float32)
    if shards:
        drawn = drawn * steps_of(stream_key, shape, shards, -0.22, 0.18)
    return jnp.clip(drawn, -reach, reach).astype(dtype)


def setup_inputs(seed: int = 0) -> dict:
    keys = jax.random.split(jax.random.key(seed), 5)
    fields = noise(keys[0], (3, H, NR, NA), 1.0, 6.0, ((2, 4), (3, 8)), jnp.float32)
    viscosity = jnp.clip(jnp.exp(math.log(0.5) - 2.3025851 * jax.random.uniform(keys[1], (NR, NA), jnp.float32) ** steps_of(keys[1], (NR, NA), ((0, 4), (1, 8)), -0.2, 0.2)), 0.05, 0.5)
    rotation = jnp.clip(jnp.exp(jax.random.uniform(keys[2], (NR,), jnp.float32, math.log(0.2), math.log(2.0))), 0.2, 2.0)
    shift_blocks = place_ends(jax.random.randint(keys[3], (STEPS, NR), 0, NB), jax.random.fold_in(keys[3], 1), 0, NB - 1).astype(jnp.int32)
    return {"fields": fields, "viscosity": viscosity, "rotation": rotation, "shift_blocks": shift_blocks}


time_step = 0.3


def rates(ext, viscosity, rotation):
    centre = ext[:, :, 1:-1, 1:-1]
    north = ext[:, :, 2:, 1:-1]
    south = ext[:, :, :-2, 1:-1]
    ahead = ext[:, :, 1:-1, 2:]
    behind = ext[:, :, 1:-1, :-2]
    above = jnp.concatenate([centre[:, 1:], centre[:, -1:]], axis=1)
    below = jnp.concatenate([centre[:, :1], centre[:, :-1]], axis=1)
    spread = viscosity * (north + south + ahead + behind + above + below - 6.0 * centre)
    radial_grad = 0.5 * (north - south)
    azimuth_grad = 0.5 * (ahead - behind)
    spin = rotation[:, None]
    rate_density = spread[0] - radial_grad[1] - azimuth_grad[2]
    rate_radial = spread[1] - radial_grad[0] + 2.0 * spin * centre[2]
    rate_azimuth = spread[2] - azimuth_grad[0] - 0.5 * spin * centre[1]
    return jnp.stack([rate_density, rate_radial, rate_azimuth])


def extend(state):
    padded = jnp.pad(state, ((0, 0), (0, 0), (1, 1), (0, 0)))
    return jnp.concatenate([padded[..., -1:], padded, padded[..., :1]], axis=3)


def advect(state, shifts):
    total = state.shape[3]
    count = total // BLOCK
    blocks = state.reshape(3, state.shape[1], state.shape[2], count, BLOCK)
    index = (lax.iota(jnp.int32, count)[None, :] - shifts.astype(jnp.int32)[:, None]) % count
    index = jnp.broadcast_to(index[None, None, :, :, None], blocks.shape).astype(jnp.int32)
    moved = jnp.take_along_axis(blocks, index, axis=3)
    return moved.reshape(state.shape)


def reference(fields, viscosity, rotation, shift_blocks):
    state = fields
    for step in range(STEPS):
        first = state + time_step * rates(extend(state), viscosity, rotation)
        second = 0.75 * state + 0.25 * (first + time_step * rates(extend(first), viscosity, rotation))
        state = state / 3.0 + (2.0 / 3.0) * (second + time_step * rates(extend(second), viscosity, rotation))
        state = advect(state, shift_blocks[step])
    return state
```

```python
import functools

import jax
import jax.numpy as jnp
from jax import lax
from jax.experimental import pallas as pl
from jax.experimental.pallas import tpu as pltpu
from jax.sharding import PartitionSpec as P

BLOCK = 64
time_step = 0.3
MESH = pl.DeviceIdType.MESH
DEPTH = 3


def neighbour_rates(centre, north, south, viscosity, spin):
    width = centre.shape[-1]
    level = lax.broadcasted_iota(jnp.int32, centre.shape, 1)
    ahead = pltpu.roll(centre, width - 1, axis=2)
    behind = pltpu.roll(centre, 1, axis=2)
    above = jnp.where(level == 7, centre, pltpu.roll(centre, 7, axis=1))
    below = jnp.where(level == 0, centre, pltpu.roll(centre, 1, axis=1))
    spread = viscosity * (north + south + ahead + behind + above + below - 6.0 * centre)
    radial_grad = 0.5 * (north - south)
    azimuth_grad = 0.5 * (ahead - behind)
    rate_density = spread[0] - radial_grad[1] - azimuth_grad[2]
    rate_radial = spread[1] - radial_grad[0] + 2.0 * spin * centre[2]
    rate_azimuth = spread[2] - azimuth_grad[0] - 0.5 * spin * centre[1]
    return jnp.stack([rate_density, rate_radial, rate_azimuth])


def kernel(
    bands, sectors, chunks,
    fields, viscosity, rotation, shifts, out,
    own, side, first, second, final, partner, lines, pack, from_ahead, from_behind,
    halo_sent, halo_got, pair_sent, pair_got, right_sent, right_got, left_sent, left_got,
):
    radii = viscosity.shape[0]
    places = sectors // 2
    band = lax.axis_index("rad")
    sector = lax.axis_index("azi")
    place, parity = sector // 2, sector % 2
    has_up, has_down = band < bands - 1, band > 0

    def at(dr, da):
        return (lax.rem(band + dr + bands, bands), lax.rem(sector + da + sectors, sectors))

    barrier = pltpu.get_barrier_semaphore()
    greeted = [(dr, da) for dr in (-1, 0, 1) for da in (-1, 0, 1) if (dr, da) != (0, 0)] + [(0, -2), (0, 2)]
    for dr, da in greeted:
        pl.semaphore_signal(barrier, inc=1, device_id=at(dr, da), device_id_type=MESH)

    lane = lax.broadcasted_iota(jnp.int32, (8, 128), 1)
    slot = ((lane + 4) // 8) % 16
    for group in range(2):
        packed = None
        for r in range(4 * group, 4 * group + 4):
            for f in range(4):
                if f < 3:
                    tile = fields[f, pl.ds(r, 8, stride=8), :]
                else:
                    tile = jnp.broadcast_to(viscosity[pl.ds(r, 1), :], (8, 128))
                own[DEPTH + r, f] = tile
                index = (r % 4) * 4 + f
                if index == 0:
                    packed = tile
                else:
                    packed = jnp.where(slot == index, pltpu.roll(tile, 8 * index, axis=1), packed)
        pack[group] = packed

    pl.semaphore_wait(barrier, len(greeted))

    def remote(src, dst, sent, got, device):
        return pltpu.make_async_remote_copy(
            src_ref=src, dst_ref=dst, send_sem=sent, recv_sem=got, device_id=device, device_id_type=MESH
        )

    def halo(index, src, dst, device):
        return remote(src, dst, halo_sent.at[index], halo_got.at[index], device)

    last = DEPTH + radii
    up = [
        halo(0, own.at[radii:last], own.at[0:DEPTH], at(1, 0)),
        halo(4, pack.at[1], from_behind.at[0, 1], at(1, 1)),
        halo(5, pack.at[1], from_ahead.at[0, 1], at(1, -1)),
    ]
    down = [
        halo(1, own.at[DEPTH:2 * DEPTH], own.at[last:last + DEPTH], at(-1, 0)),
        halo(6, pack.at[0], from_behind.at[2, 0], at(-1, 1)),
        halo(7, pack.at[0], from_ahead.at[2, 0], at(-1, -1)),
    ]
    across = [
        halo(2, pack, from_behind.at[1], at(0, 1)),
        halo(3, pack, from_ahead.at[1], at(0, -1)),
    ]
    for copy in across:
        copy.start()

    @pl.when(has_up)
    def _():
        for copy in up:
            copy.start()

    @pl.when(has_down)
    def _():
        for copy in down:
            copy.start()

    low = (lane % 8) < 4

    def unpack(dr, group, rows, shift):
        joined = jnp.where(low, from_ahead[dr, group], from_behind[dr, group])
        for r in rows:
            for f in range(4):
                index = (r % 4) * 4 + f
                side[shift + r, f] = joined if index == 0 else pltpu.roll(joined, 128 - 8 * index, axis=1)

    for copy in across:
        copy.wait_recv()
    unpack(1, 0, range(0, 4), DEPTH)
    unpack(1, 1, range(4, 8), DEPTH)

    @pl.when(has_down)
    def _():
        for copy in up:
            copy.wait_recv()
        unpack(0, 1, range(radii - DEPTH, radii), DEPTH - radii)

    @pl.when(jnp.logical_not(has_down))
    def _():
        own[0:DEPTH] = jnp.zeros((DEPTH, 4, 8, 128), jnp.float32)
        side[0:DEPTH] = jnp.zeros((DEPTH, 4, 8, 128), jnp.float32)

    @pl.when(has_up)
    def _():
        for copy in down:
            copy.wait_recv()
        unpack(2, 0, range(0, DEPTH), last)

    @pl.when(jnp.logical_not(has_up))
    def _():
        own[last:last + DEPTH] = jnp.zeros((DEPTH, 4, 8, 128), jnp.float32)
        side[last:last + DEPTH] = jnp.zeros((DEPTH, 4, 8, 128), jnp.float32)

    def start_row(i):
        return jnp.concatenate([own[i, 0:3], side[i, 0:3]], axis=2)

    def row_facts(i):
        row = band * radii + i - DEPTH
        inside = jnp.logical_and(row >= 0, row < bands * radii)
        spin = rotation[jnp.clip(row, 0, bands * radii - 1)]
        return inside, spin, jnp.concatenate([own[i, 3], side[i, 3]], axis=1)

    def first_row(i, _):
        inside, spin, thick = row_facts(i)
        centre = start_row(i)
        rate = neighbour_rates(centre, start_row(i + 1), start_row(i - 1), thick, spin)
        first[i] = jnp.where(inside, centre + time_step * rate, 0.0)
        return 0

    lax.fori_loop(1, radii + 2 * DEPTH - 1, first_row, 0, unroll=True)

    def second_row(i, _):
        inside, spin, thick = row_facts(i)
        centre = first[i]
        rate = neighbour_rates(centre, first[i + 1], first[i - 1], thick, spin)
        second[i] = jnp.where(inside, 0.75 * start_row(i) + 0.25 * (centre + time_step * rate), 0.0)
        return 0

    lax.fori_loop(2, radii + 2 * DEPTH - 2, second_row, 0, unroll=True)

    def final_row(r, _):
        i = r + DEPTH
        inside, spin, thick = row_facts(i)
        centre = second[i]
        rate = neighbour_rates(centre, second[i + 1], second[i - 1], thick, spin)
        final[r] = own[i, 0:3] / 3.0 + 2.0 / 3.0 * (centre + time_step * rate)[..., :128]
        return 0

    per = radii // chunks

    def rows_of(c):
        return pl.ds(c * per, per)

    def pair_copy(c):
        mate = (band, sector + 1 - 2 * parity)
        return remote(final.at[rows_of(c)], partner.at[rows_of(c)], pair_sent.at[c], pair_got.at[c], mate)

    for c in range(chunks):
        lax.fori_loop(c * per, (c + 1) * per, final_row, 0, unroll=True)
        pair_copy(c).start()

    half = lax.broadcasted_iota(jnp.int32, (3, 8, 128), 2) < BLOCK

    def join_row(r):
        shift = shifts[0, band * radii + r]
        here, there = final[r], partner[r]
        left_own = (2 * parity - shift + 2 * sectors) % 4 // 2 == parity
        right_own = (2 * parity + 1 - shift + 2 * sectors) % 4 // 2 == parity
        odd = shift % 2 == 1
        here = jnp.where(odd, pltpu.roll(here, BLOCK, axis=2), here)
        there = jnp.where(odd, pltpu.roll(there, BLOCK, axis=2), there)
        take = jnp.where(half, left_own.astype(jnp.int32), right_own.astype(jnp.int32))
        lines[r // per][place, r % per] = jnp.where(take == 1, here, there)

    def line_copy(to_right, k, c):
        if to_right:
            held = lines[c].at[jnp.maximum(place - k, 0)]
            return remote(held, held, right_sent.at[k, c], right_got.at[k, c], at(0, 2))
        held = lines[c].at[jnp.minimum(place + k, places - 1)]
        return remote(held, held, left_sent.at[k, c], left_got.at[k, c], at(0, -2))

    def sends(to_right, k):
        if to_right:
            return jnp.logical_and(place < places - 1, place - k >= 0)
        return jnp.logical_and(place > 0, place + k < places)

    def gets(to_right, k):
        if to_right:
            return place - 1 - k >= 0
        return place + 1 + k < places

    def send(k, c):
        for to_right in (True, False):
            @pl.when(sends(to_right, k))
            def _():
                line_copy(to_right, k, c).start()

    def get(k, c):
        for to_right in (True, False):
            @pl.when(gets(to_right, k))
            def _():
                line_copy(to_right, k, c).wait_recv()

    for c in range(chunks):
        pair_copy(c).wait_recv()
        for r in range(c * per, (c + 1) * per):
            join_row(r)
        send(0, c)

    def forward(k, _):
        for c in range(chunks):
            get(k - 1, c)
            send(k, c)
        return 0

    if places <= 4:
        for k in range(1, places - 1):
            forward(k, 0)
    else:
        lax.fori_loop(1, places - 1, forward, 0)

    for c in range(chunks):
        if places > 1:
            get(places - 2, c)
        for r in range(c * per, (c + 1) * per):
            shift = shifts[0, band * radii + r]
            total = 2 * sectors
            left_from = (2 * sector - shift + total) % total // 4
            right_from = (2 * sector + 1 - shift + total) % total // 4
            moved = jnp.where(half, lines[c][left_from, r % per], lines[c][right_from, r % per])
            for f in range(3):
                out[f, pl.ds(r, 8, stride=8), :] = moved[f]

    for copy in across:
        copy.wait_send()

    @pl.when(has_up)
    def _():
        for copy in up:
            copy.wait_send()

    @pl.when(has_down)
    def _():
        for copy in down:
            copy.wait_send()

    for c in range(chunks):
        pair_copy(c).wait_send()

    def settle(k, _):
        for c in range(chunks):
            for to_right in (True, False):
                @pl.when(sends(to_right, k))
                def _():
                    line_copy(to_right, k, c).wait_send()
        return 0

    if places <= 4:
        for k in range(places - 1):
            settle(k, 0)
    else:
        lax.fori_loop(0, places - 1, settle, 0)


def body(fields, viscosity, rotation, shift_blocks):
    bands, sectors = lax.axis_size("rad"), lax.axis_size("azi")
    kinds, height, radii, width = fields.shape
    places, chunks = sectors // 2, 4
    rows = radii + 2 * DEPTH
    steps = max(places - 1, 1)
    vmem = lambda *shape: pltpu.VMEM(shape, jnp.float32)
    dma = lambda *shape: pltpu.SemaphoreType.DMA(shape)
    moved = pl.pallas_call(
        functools.partial(kernel, bands, sectors, chunks),
        out_shape=jax.ShapeDtypeStruct((kinds, height * radii, width), jnp.float32),
        in_specs=[
            pl.BlockSpec(memory_space=pltpu.VMEM),
            pl.BlockSpec(memory_space=pltpu.VMEM),
            pl.BlockSpec(memory_space=pltpu.SMEM),
            pl.BlockSpec(memory_space=pltpu.SMEM),
        ],
        out_specs=pl.BlockSpec(memory_space=pltpu.VMEM),
        scratch_shapes=[
            vmem(rows, 4, 8, 128), vmem(rows, 4, 8, 128),
            vmem(rows, 3, 8, 256), vmem(rows, 3, 8, 256),
            vmem(radii, 3, 8, 128), vmem(radii, 3, 8, 128),
            [vmem(places, radii // chunks, 3, 8, 128) for _ in range(chunks)],
            vmem(2, 8, 128), vmem(3, 2, 8, 128), vmem(3, 2, 8, 128),
            dma(8), dma(8), dma(chunks), dma(chunks),
            dma(steps, chunks), dma(steps, chunks), dma(steps, chunks), dma(steps, chunks),
        ],
        compiler_params=pltpu.CompilerParams(collective_id=0, has_side_effects=True, vmem_limit_bytes=24 * 2**20),
        name="disc_step",
    )(fields.reshape(kinds, height * radii, width), viscosity, rotation, shift_blocks)
    return moved.reshape(fields.shape)


def solution(mesh):
    return jax.shard_map(
        body,
        mesh=mesh,
        in_specs=(P(None, None, "rad", "azi"), P("rad", "azi"), P(), P()),
        out_specs=P(None, None, "rad", "azi"),
        check_vma=False,
    )
```

```python
import functools

import jax
import jax.numpy as jnp
from jax import lax
from jax.experimental import pallas as pl
from jax.experimental.pallas import tpu as pltpu
from jax.sharding import PartitionSpec as P

BLOCK = 64
time_step = 0.3
MESH = pl.DeviceIdType.MESH
DEPTH = 3


def neighbour_rates(centre, north, south, viscosity, spin):
    width = centre.shape[-1]
    level = lax.broadcasted_iota(jnp.int32, centre.shape, 1)
    ahead = pltpu.roll(centre, width - 1, axis=2)
    behind = pltpu.roll(centre, 1, axis=2)
    above = jnp.where(level == 7, centre, pltpu.roll(centre, 7, axis=1))
    below = jnp.where(level == 0, centre, pltpu.roll(centre, 1, axis=1))
    spread = viscosity * (north + south + ahead + behind + above + below - 6.0 * centre)
    radial_grad = 0.5 * (north - south)
    azimuth_grad = 0.5 * (ahead - behind)
    rate_density = spread[0] - radial_grad[1] - azimuth_grad[2]
    rate_radial = spread[1] - radial_grad[0] + 2.0 * spin * centre[2]
    rate_azimuth = spread[2] - azimuth_grad[0] - 0.5 * spin * centre[1]
    return jnp.stack([rate_density, rate_radial, rate_azimuth])


def kernel(
    bands, sectors, chunks,
    fields_in, viscosity_in, rotation_in, shifts_in, out,
    fields, viscosity, rotation, shifts, fetched, own, side, first, second, final, partner, lines, pack, from_ahead, from_behind,
    halo_sent, halo_got, pair_sent, pair_got, right_sent, right_got, left_sent, left_got,
):
    radii = viscosity.shape[0]
    places = sectors // 2
    band = lax.axis_index("rad")
    sector = lax.axis_index("azi")
    place, parity = sector // 2, sector % 2
    has_up, has_down = band < bands - 1, band > 0

    def at(dr, da):
        return (lax.rem(band + dr + bands, bands), lax.rem(sector + da + sectors, sectors))

    barrier = pltpu.get_barrier_semaphore()
    greeted = [(dr, da) for dr in (-1, 0, 1) for da in (-1, 0, 1) if (dr, da) != (0, 0)] + [(0, -2), (0, 2)]
    for dr, da in greeted:
        pl.semaphore_signal(barrier, inc=1, device_id=at(dr, da), device_id_type=MESH)

    fetches = [
        pltpu.make_async_copy(src, dst, fetched.at[i])
        for i, (src, dst) in enumerate(
            [(fields_in, fields), (viscosity_in, viscosity), (rotation_in, rotation), (shifts_in, shifts)]
        )
    ]
    for fetch in fetches:
        fetch.start()
    for fetch in fetches:
        fetch.wait()

    lane = lax.broadcasted_iota(jnp.int32, (8, 128), 1)
    slot = ((lane + 4) // 8) % 16
    for group in range(2):
        packed = None
        for r in range(4 * group, 4 * group + 4):
            for f in range(4):
                if f < 3:
                    tile = fields[f, pl.ds(r, 8, stride=8), :]
                else:
                    tile = jnp.broadcast_to(viscosity[pl.ds(r, 1), :], (8, 128))
                own[DEPTH + r, f] = tile
                index = (r % 4) * 4 + f
                if index == 0:
                    packed = tile
                else:
                    packed = jnp.where(slot == index, pltpu.roll(tile, 8 * index, axis=1), packed)
        pack[group] = packed

    pl.semaphore_wait(barrier, len(greeted))

    def remote(src, dst, sent, got, device):
        return pltpu.make_async_remote_copy(
            src_ref=src, dst_ref=dst, send_sem=sent, recv_sem=got, device_id=device, device_id_type=MESH
        )

    def halo(index, src, dst, device):
        return remote(src, dst, halo_sent.at[index], halo_got.at[index], device)

    last = DEPTH + radii
    up = [
        halo(0, own.at[radii:last], own.at[0:DEPTH], at(1, 0)),
        halo(4, pack.at[1], from_behind.at[0, 1], at(1, 1)),
        halo(5, pack.at[1], from_ahead.at[0, 1], at(1, -1)),
    ]
    down = [
        halo(1, own.at[DEPTH:2 * DEPTH], own.at[last:last + DEPTH], at(-1, 0)),
        halo(6, pack.at[0], from_behind.at[2, 0], at(-1, 1)),
        halo(7, pack.at[0], from_ahead.at[2, 0], at(-1, -1)),
    ]
    across = [
        halo(2, pack, from_behind.at[1], at(0, 1)),
        halo(3, pack, from_ahead.at[1], at(0, -1)),
    ]
    for copy in across:
        copy.start()

    @pl.when(has_up)
    def _():
        for copy in up:
            copy.start()

    @pl.when(has_down)
    def _():
        for copy in down:
            copy.start()

    low = (lane % 8) < 4

    def unpack(dr, group, rows, shift):
        joined = jnp.where(low, from_ahead[dr, group], from_behind[dr, group])
        for r in rows:
            for f in range(4):
                index = (r % 4) * 4 + f
                side[shift + r, f] = joined if index == 0 else pltpu.roll(joined, 128 - 8 * index, axis=1)

    for copy in across:
        copy.wait_recv()
    unpack(1, 0, range(0, 4), DEPTH)
    unpack(1, 1, range(4, 8), DEPTH)

    @pl.when(has_down)
    def _():
        for copy in up:
            copy.wait_recv()
        unpack(0, 1, range(radii - DEPTH, radii), DEPTH - radii)

    @pl.when(jnp.logical_not(has_down))
    def _():
        own[0:DEPTH] = jnp.zeros((DEPTH, 4, 8, 128), jnp.float32)
        side[0:DEPTH] = jnp.zeros((DEPTH, 4, 8, 128), jnp.float32)

    @pl.when(has_up)
    def _():
        for copy in down:
            copy.wait_recv()
        unpack(2, 0, range(0, DEPTH), last)

    @pl.when(jnp.logical_not(has_up))
    def _():
        own[last:last + DEPTH] = jnp.zeros((DEPTH, 4, 8, 128), jnp.float32)
        side[last:last + DEPTH] = jnp.zeros((DEPTH, 4, 8, 128), jnp.float32)

    def start_row(i):
        return jnp.concatenate([own[i, 0:3], side[i, 0:3]], axis=2)

    def row_facts(i):
        row = band * radii + i - DEPTH
        inside = jnp.logical_and(row >= 0, row < bands * radii)
        spin = rotation[jnp.clip(row, 0, bands * radii - 1)]
        return inside, spin, jnp.concatenate([own[i, 3], side[i, 3]], axis=1)

    def first_row(i, _):
        inside, spin, thick = row_facts(i)
        centre = start_row(i)
        rate = neighbour_rates(centre, start_row(i + 1), start_row(i - 1), thick, spin)
        first[i] = jnp.where(inside, centre + time_step * rate, 0.0)
        return 0

    lax.fori_loop(1, radii + 2 * DEPTH - 1, first_row, 0, unroll=True)

    def second_row(i, _):
        inside, spin, thick = row_facts(i)
        centre = first[i]
        rate = neighbour_rates(centre, first[i + 1], first[i - 1], thick, spin)
        second[i] = jnp.where(inside, 0.75 * start_row(i) + 0.25 * (centre + time_step * rate), 0.0)
        return 0

    lax.fori_loop(2, radii + 2 * DEPTH - 2, second_row, 0, unroll=True)

    def final_row(r, _):
        i = r + DEPTH
        inside, spin, thick = row_facts(i)
        centre = second[i]
        rate = neighbour_rates(centre, second[i + 1], second[i - 1], thick, spin)
        final[r] = own[i, 0:3] / 3.0 + 2.0 / 3.0 * (centre + time_step * rate)[..., :128]
        return 0

    per = radii // chunks

    def rows_of(c):
        return pl.ds(c * per, per)

    def pair_copy(c):
        mate = (band, sector + 1 - 2 * parity)
        return remote(final.at[rows_of(c)], partner.at[rows_of(c)], pair_sent.at[c], pair_got.at[c], mate)

    for c in range(chunks):
        lax.fori_loop(c * per, (c + 1) * per, final_row, 0, unroll=True)
        pair_copy(c).start()

    half = lax.broadcasted_iota(jnp.int32, (3, 8, 128), 2) < BLOCK

    def join_row(r):
        shift = shifts[0, band * radii + r]
        here, there = final[r], partner[r]
        left_own = (2 * parity - shift + 2 * sectors) % 4 // 2 == parity
        right_own = (2 * parity + 1 - shift + 2 * sectors) % 4 // 2 == parity
        odd = shift % 2 == 1
        here = jnp.where(odd, pltpu.roll(here, BLOCK, axis=2), here)
        there = jnp.where(odd, pltpu.roll(there, BLOCK, axis=2), there)
        take = jnp.where(half, left_own.astype(jnp.int32), right_own.astype(jnp.int32))
        lines[r // per][place, r % per] = jnp.where(take == 1, here, there)

    def line_copy(to_right, k, c):
        if to_right:
            held = lines[c].at[jnp.maximum(place - k, 0)]
            return remote(held, held, right_sent.at[k, c], right_got.at[k, c], at(0, 2))
        held = lines[c].at[jnp.minimum(place + k, places - 1)]
        return remote(held, held, left_sent.at[k, c], left_got.at[k, c], at(0, -2))

    def sends(to_right, k):
        if to_right:
            return jnp.logical_and(place < places - 1, place - k >= 0)
        return jnp.logical_and(place > 0, place + k < places)

    def gets(to_right, k):
        if to_right:
            return place - 1 - k >= 0
        return place + 1 + k < places

    def send(k, c):
        for to_right in (True, False):
            @pl.when(sends(to_right, k))
            def _():
                line_copy(to_right, k, c).start()

    def get(k, c):
        for to_right in (True, False):
            @pl.when(gets(to_right, k))
            def _():
                line_copy(to_right, k, c).wait_recv()

    for c in range(chunks):
        pair_copy(c).wait_recv()
        for r in range(c * per, (c + 1) * per):
            join_row(r)
        send(0, c)

    def forward(k, _):
        for c in range(chunks):
            get(k - 1, c)
            send(k, c)
        return 0

    if places <= 4:
        for k in range(1, places - 1):
            forward(k, 0)
    else:
        lax.fori_loop(1, places - 1, forward, 0)

    for c in range(chunks):
        if places > 1:
            get(places - 2, c)
        for r in range(c * per, (c + 1) * per):
            shift = shifts[0, band * radii + r]
            total = 2 * sectors
            left_from = (2 * sector - shift + total) % total // 4
            right_from = (2 * sector + 1 - shift + total) % total // 4
            moved = jnp.where(half, lines[c][left_from, r % per], lines[c][right_from, r % per])
            for f in range(3):
                out[f, pl.ds(r, 8, stride=8), :] = moved[f]

    for copy in across:
        copy.wait_send()

    @pl.when(has_up)
    def _():
        for copy in up:
            copy.wait_send()

    @pl.when(has_down)
    def _():
        for copy in down:
            copy.wait_send()

    for c in range(chunks):
        pair_copy(c).wait_send()

    def settle(k, _):
        for c in range(chunks):
            for to_right in (True, False):
                @pl.when(sends(to_right, k))
                def _():
                    line_copy(to_right, k, c).wait_send()
        return 0

    if places <= 4:
        for k in range(places - 1):
            settle(k, 0)
    else:
        lax.fori_loop(0, places - 1, settle, 0)


def body(fields, viscosity, rotation, shift_blocks):
    bands, sectors = lax.axis_size("rad"), lax.axis_size("azi")
    kinds, height, radii, width = fields.shape
    places, chunks = sectors // 2, 4
    rows = radii + 2 * DEPTH
    steps = max(places - 1, 1)
    vmem = lambda *shape: pltpu.VMEM(shape, jnp.float32)
    dma = lambda *shape: pltpu.SemaphoreType.DMA(shape)
    moved = pl.pallas_call(
        functools.partial(kernel, bands, sectors, chunks),
        out_shape=jax.ShapeDtypeStruct((kinds, height * radii, width), jnp.float32),
        in_specs=[pl.BlockSpec(memory_space=pltpu.HBM)] * 4,
        out_specs=pl.BlockSpec(memory_space=pltpu.VMEM),
        scratch_shapes=[
            vmem(kinds, height * radii, width), vmem(radii, width),
            pltpu.SMEM(rotation.shape, jnp.float32), pltpu.SMEM(shift_blocks.shape, jnp.int32), dma(4),
            vmem(rows, 4, 8, 128), vmem(rows, 4, 8, 128),
            vmem(rows, 3, 8, 256), vmem(rows, 3, 8, 256),
            vmem(radii, 3, 8, 128), vmem(radii, 3, 8, 128),
            [vmem(places, radii // chunks, 3, 8, 128) for _ in range(chunks)],
            vmem(2, 8, 128), vmem(3, 2, 8, 128), vmem(3, 2, 8, 128),
            dma(8), dma(8), dma(chunks), dma(chunks),
            dma(steps, chunks), dma(steps, chunks), dma(steps, chunks), dma(steps, chunks),
        ],
        compiler_params=pltpu.CompilerParams(collective_id=0, has_side_effects=True, vmem_limit_bytes=56 * 2**20),
        name="disc_step",
    )(fields.reshape(kinds, height * radii, width), viscosity, rotation, shift_blocks)
    return moved.reshape(fields.shape)


def solution(mesh):
    return jax.shard_map(
        body,
        mesh=mesh,
        in_specs=(P(None, None, "rad", "azi"), P("rad", "azi"), P(), P()),
        out_specs=P(None, None, "rad", "azi"),
        check_vma=False,
    )
```

```python
import functools

import jax
import jax.numpy as jnp
from jax import lax
from jax.experimental import pallas as pl
from jax.experimental.pallas import tpu as pltpu
from jax.sharding import PartitionSpec as P

BLOCK = 64
time_step = 0.3
MESH = pl.DeviceIdType.MESH
DEPTH = 3


def neighbour_rates(centre, north, south, viscosity, spin):
    width = centre.shape[-1]
    level = lax.broadcasted_iota(jnp.int32, centre.shape, 1)
    ahead = pltpu.roll(centre, width - 1, axis=2)
    behind = pltpu.roll(centre, 1, axis=2)
    above = jnp.where(level == 7, centre, pltpu.roll(centre, 7, axis=1))
    below = jnp.where(level == 0, centre, pltpu.roll(centre, 1, axis=1))
    spread = viscosity * (north + south + ahead + behind + above + below - 6.0 * centre)
    radial_grad = 0.5 * (north - south)
    azimuth_grad = 0.5 * (ahead - behind)
    rate_density = spread[0] - radial_grad[1] - azimuth_grad[2]
    rate_radial = spread[1] - radial_grad[0] + 2.0 * spin * centre[2]
    rate_azimuth = spread[2] - azimuth_grad[0] - 0.5 * spin * centre[1]
    return jnp.stack([rate_density, rate_radial, rate_azimuth])


def kernel(
    bands, sectors, chunks,
    fields_in, viscosity_in, rotation_in, shifts_in, out,
    fields, viscosity, rotation, shifts, fetched, own, side, first, second, final, partner, lefts, rights, merged, pack, from_ahead, from_behind,
    halo_sent, halo_got, pair_sent, pair_got, right_sent, right_got, left_sent, left_got,
):
    radii = viscosity.shape[0]
    places = sectors // 2
    band = lax.axis_index("rad")
    sector = lax.axis_index("azi")
    place, parity = sector // 2, sector % 2
    has_up, has_down = band < bands - 1, band > 0

    def at(dr, da):
        return (lax.rem(band + dr + bands, bands), lax.rem(sector + da + sectors, sectors))

    barrier = pltpu.get_barrier_semaphore()
    greeted = [(dr, da) for dr in (-1, 0, 1) for da in (-1, 0, 1) if (dr, da) != (0, 0)] + [(0, -2), (0, 2)]
    for dr, da in greeted:
        pl.semaphore_signal(barrier, inc=1, device_id=at(dr, da), device_id_type=MESH)

    fetches = [
        pltpu.make_async_copy(src, dst, fetched.at[i])
        for i, (src, dst) in enumerate(
            [(fields_in, fields), (viscosity_in, viscosity), (rotation_in, rotation), (shifts_in, shifts)]
        )
    ]
    for fetch in fetches:
        fetch.start()
    for fetch in fetches:
        fetch.wait()

    lane = lax.broadcasted_iota(jnp.int32, (8, 128), 1)
    slot = ((lane + 4) // 8) % 16
    for group in range(2):
        packed = None
        for r in range(4 * group, 4 * group + 4):
            for f in range(4):
                if f < 3:
                    tile = fields[f, pl.ds(r, 8, stride=8), :]
                else:
                    tile = jnp.broadcast_to(viscosity[pl.ds(r, 1), :], (8, 128))
                own[DEPTH + r, f] = tile
                index = (r % 4) * 4 + f
                if index == 0:
                    packed = tile
                else:
                    packed = jnp.where(slot == index, pltpu.roll(tile, 8 * index, axis=1), packed)
        pack[group] = packed

    pl.semaphore_wait(barrier, len(greeted))

    def remote(src, dst, sent, got, device):
        return pltpu.make_async_remote_copy(
            src_ref=src, dst_ref=dst, send_sem=sent, recv_sem=got, device_id=device, device_id_type=MESH
        )

    def halo(index, src, dst, device):
        return remote(src, dst, halo_sent.at[index], halo_got.at[index], device)

    last = DEPTH + radii
    up = [
        halo(0, own.at[radii:last], own.at[0:DEPTH], at(1, 0)),
        halo(4, pack.at[1], from_behind.at[0, 1], at(1, 1)),
        halo(5, pack.at[1], from_ahead.at[0, 1], at(1, -1)),
    ]
    down = [
        halo(1, own.at[DEPTH:2 * DEPTH], own.at[last:last + DEPTH], at(-1, 0)),
        halo(6, pack.at[0], from_behind.at[2, 0], at(-1, 1)),
        halo(7, pack.at[0], from_ahead.at[2, 0], at(-1, -1)),
    ]
    across = [
        halo(2, pack, from_behind.at[1], at(0, 1)),
        halo(3, pack, from_ahead.at[1], at(0, -1)),
    ]
    for copy in across:
        copy.start()

    @pl.when(has_up)
    def _():
        for copy in up:
            copy.start()

    @pl.when(has_down)
    def _():
        for copy in down:
            copy.start()

    low = (lane % 8) < 4

    def unpack(dr, group, rows, shift):
        joined = jnp.where(low, from_ahead[dr, group], from_behind[dr, group])
        for r in rows:
            for f in range(4):
                index = (r % 4) * 4 + f
                side[shift + r, f] = joined if index == 0 else pltpu.roll(joined, 128 - 8 * index, axis=1)

    for copy in across:
        copy.wait_recv()
    unpack(1, 0, range(0, 4), DEPTH)
    unpack(1, 1, range(4, 8), DEPTH)

    @pl.when(has_down)
    def _():
        for copy in up:
            copy.wait_recv()
        unpack(0, 1, range(radii - DEPTH, radii), DEPTH - radii)

    @pl.when(jnp.logical_not(has_down))
    def _():
        own[0:DEPTH] = jnp.zeros((DEPTH, 4, 8, 128), jnp.float32)
        side[0:DEPTH] = jnp.zeros((DEPTH, 4, 8, 128), jnp.float32)

    @pl.when(has_up)
    def _():
        for copy in down:
            copy.wait_recv()
        unpack(2, 0, range(0, DEPTH), last)

    @pl.when(jnp.logical_not(has_up))
    def _():
        own[last:last + DEPTH] = jnp.zeros((DEPTH, 4, 8, 128), jnp.float32)
        side[last:last + DEPTH] = jnp.zeros((DEPTH, 4, 8, 128), jnp.float32)

    def start_row(i):
        return jnp.concatenate([own[i, 0:3], side[i, 0:3]], axis=2)

    def row_facts(i):
        row = band * radii + i - DEPTH
        inside = jnp.logical_and(row >= 0, row < bands * radii)
        spin = rotation[jnp.clip(row, 0, bands * radii - 1)]
        return inside, spin, jnp.concatenate([own[i, 3], side[i, 3]], axis=1)

    def first_row(i, _):
        inside, spin, thick = row_facts(i)
        centre = start_row(i)
        rate = neighbour_rates(centre, start_row(i + 1), start_row(i - 1), thick, spin)
        first[i] = jnp.where(inside, centre + time_step * rate, 0.0)
        return 0

    lax.fori_loop(1, radii + 2 * DEPTH - 1, first_row, 0, unroll=True)

    def second_row(i, _):
        inside, spin, thick = row_facts(i)
        centre = first[i]
        rate = neighbour_rates(centre, first[i + 1], first[i - 1], thick, spin)
        second[i] = jnp.where(inside, 0.75 * start_row(i) + 0.25 * (centre + time_step * rate), 0.0)
        return 0

    lax.fori_loop(2, radii + 2 * DEPTH - 2, second_row, 0, unroll=True)

    def final_row(r, _):
        i = r + DEPTH
        inside, spin, thick = row_facts(i)
        centre = second[i]
        rate = neighbour_rates(centre, second[i + 1], second[i - 1], thick, spin)
        final[r] = own[i, 0:3] / 3.0 + 2.0 / 3.0 * (centre + time_step * rate)[..., :128]
        return 0

    per = radii // chunks

    def rows_of(c):
        return pl.ds(c * per, per)

    def pair_copy(c):
        mate = (band, sector + 1 - 2 * parity)
        return remote(final.at[rows_of(c)], partner.at[rows_of(c)], pair_sent.at[c], pair_got.at[c], mate)

    for c in range(chunks):
        lax.fori_loop(c * per, (c + 1) * per, final_row, 0, unroll=True)
        pair_copy(c).start()

    half = lax.broadcasted_iota(jnp.int32, (3, 8, 128), 2) < BLOCK

    def join_row(r):
        shift = shifts[0, band * radii + r]
        here, there = final[r], partner[r]
        left_own = (2 * parity - shift + 2 * sectors) % 4 // 2 == parity
        right_own = (2 * parity + 1 - shift + 2 * sectors) % 4 // 2 == parity
        odd = shift % 2 == 1
        here = jnp.where(odd, pltpu.roll(here, BLOCK, axis=2), here)
        there = jnp.where(odd, pltpu.roll(there, BLOCK, axis=2), there)
        take = jnp.where(half, left_own.astype(jnp.int32), right_own.astype(jnp.int32))
        joined = jnp.where(take == 1, here, there)
        lefts[r // per][place, r % per] = joined
        rights[r // per][place, r % per] = joined

    def line_copy(to_right, k, c):
        if to_right:
            held = lefts[c].at[jnp.maximum(place - k, 0)]
            return remote(held, held, right_sent.at[k, c], right_got.at[k, c], at(0, 2))
        held = rights[c].at[jnp.minimum(place + k, places - 1)]
        return remote(held, held, left_sent.at[k, c], left_got.at[k, c], at(0, -2))

    def end_copy(to_right, c):
        if to_right:
            return remote(merged.at[0, c], lefts[c].at[place], right_sent.at[0, c], right_got.at[0, c], at(0, 2))
        return remote(merged.at[1, c], rights[c].at[place], left_sent.at[0, c], left_got.at[0, c], at(0, -2))

    def ends(to_right):
        return place == places - 2 if to_right else place == 1

    def sends(to_right, k):
        if to_right:
            return jnp.logical_and(place < places - 2, place - k >= 0)
        return jnp.logical_and(place > 1, place + k < places)

    def gets(to_right, k):
        if to_right:
            return jnp.logical_and(place < places - 1, place - 1 - k >= 0)
        return jnp.logical_and(place > 0, place + 1 + k < places)

    def gets_end(to_right):
        return place == places - 1 if to_right else place == 0

    def send(k, c):
        for to_right in (True, False):
            @pl.when(sends(to_right, k))
            def _():
                line_copy(to_right, k, c).start()

    def get(k, c):
        for to_right in (True, False):
            @pl.when(gets(to_right, k))
            def _():
                line_copy(to_right, k, c).wait_recv()

    def sources(r, target):
        shift = shifts[0, band * radii + r]
        total = 2 * sectors
        return [(2 * target + h - shift + total) % total // 4 for h in range(2)]

    def send_end(c):
        for to_right in (True, False):
            @pl.when(ends(to_right))
            def _():
                for r in range(c * per, (c + 1) * per):
                    target = sector + 2 if to_right else sector - 2
                    first_from, second_from = sources(r, target)
                    if to_right:
                        pick = lambda at_place: lefts[c][jnp.minimum(at_place, place), r % per]
                    else:
                        pick = lambda at_place: rights[c][jnp.maximum(at_place, place), r % per]
                    merged[1 - int(to_right), c, r % per] = jnp.where(half, pick(first_from), pick(second_from))
                end_copy(to_right, c).start()

    for c in range(chunks):
        pair_copy(c).wait_recv()
        for r in range(c * per, (c + 1) * per):
            join_row(r)
        send(0, c)

    def forward(k, _):
        for c in range(chunks):
            get(k - 1, c)
            send(k, c)
        return 0

    if places <= 4:
        for k in range(1, places - 2):
            forward(k, 0)
    else:
        lax.fori_loop(1, places - 2, forward, 0)

    for c in range(chunks):
        get(places - 3, c)
        send_end(c)

    for c in range(chunks):
        for to_right in (True, False):
            @pl.when(gets_end(to_right))
            def _():
                end_copy(to_right, c).wait_recv()
        for r in range(c * per, (c + 1) * per):
            def pick(at_place):
                near = jnp.where(place == places - 1, places - 2, at_place)
                left = jnp.where(at_place >= place, place, near)
                far = jnp.where(place == 0, 1, at_place)
                right = jnp.where(at_place <= place, place, far)
                return jnp.where(at_place <= place, lefts[c][left, r % per], rights[c][right, r % per])

            first_from, second_from = sources(r, sector)
            moved = jnp.where(half, pick(first_from), pick(second_from))
            for f in range(3):
                out[f, pl.ds(r, 8, stride=8), :] = moved[f]

    for copy in across:
        copy.wait_send()

    @pl.when(has_up)
    def _():
        for copy in up:
            copy.wait_send()

    @pl.when(has_down)
    def _():
        for copy in down:
            copy.wait_send()

    for c in range(chunks):
        pair_copy(c).wait_send()

    for c in range(chunks):
        for to_right in (True, False):
            @pl.when(ends(to_right))
            def _():
                end_copy(to_right, c).wait_send()

    def settle(k, _):
        for c in range(chunks):
            for to_right in (True, False):
                @pl.when(sends(to_right, k))
                def _():
                    line_copy(to_right, k, c).wait_send()
        return 0

    if places <= 4:
        for k in range(places - 2):
            settle(k, 0)
    else:
        lax.fori_loop(0, places - 2, settle, 0)


def body(fields, viscosity, rotation, shift_blocks):
    bands, sectors = lax.axis_size("rad"), lax.axis_size("azi")
    kinds, height, radii, width = fields.shape
    places, chunks = sectors // 2, 4
    rows = radii + 2 * DEPTH
    steps = places - 2
    vmem = lambda *shape: pltpu.VMEM(shape, jnp.float32)
    dma = lambda *shape: pltpu.SemaphoreType.DMA(shape)
    moved = pl.pallas_call(
        functools.partial(kernel, bands, sectors, chunks),
        out_shape=pltpu.VMEM((kinds, height * radii, width), jnp.float32),
        in_specs=[pl.BlockSpec(memory_space=pltpu.HBM)] * 4,
        out_specs=pl.BlockSpec(memory_space=pltpu.VMEM),
        scratch_shapes=[
            vmem(kinds, height * radii, width), vmem(radii, width),
            pltpu.SMEM(rotation.shape, jnp.float32), pltpu.SMEM(shift_blocks.shape, jnp.int32), dma(4),
            vmem(rows, 4, 8, 128), vmem(rows, 4, 8, 128),
            vmem(rows, 3, 8, 256), vmem(rows, 3, 8, 256),
            vmem(radii, 3, 8, 128), vmem(radii, 3, 8, 128),
            [vmem(places, radii // chunks, 3, 8, 128) for _ in range(chunks)],
            [vmem(places, radii // chunks, 3, 8, 128) for _ in range(chunks)],
            vmem(2, chunks, radii // chunks, 3, 8, 128),
            vmem(2, 8, 128), vmem(3, 2, 8, 128), vmem(3, 2, 8, 128),
            dma(8), dma(8), dma(chunks), dma(chunks),
            dma(steps, chunks), dma(steps, chunks), dma(steps, chunks), dma(steps, chunks),
        ],
        compiler_params=pltpu.CompilerParams(collective_id=0, has_side_effects=True, vmem_limit_bytes=56 * 2**20),
        name="disc_step",
    )(fields.reshape(kinds, height * radii, width), viscosity, rotation, shift_blocks)
    return moved.reshape(fields.shape)


def solution(mesh):
    return jax.shard_map(
        body,
        mesh=mesh,
        in_specs=(P(None, None, "rad", "azi"), P("rad", "azi"), P(), P()),
        out_specs=P(None, None, "rad", "azi"),
        check_vma=False,
    )
```

```python
import functools

import jax
import jax.numpy as jnp
from jax import lax
from jax.experimental import pallas as pl
from jax.experimental.pallas import tpu as pltpu
from jax.sharding import PartitionSpec as P

BLOCK = 64
time_step = 0.3
MESH = pl.DeviceIdType.MESH
DEPTH = 3


def neighbour_rates(centre, north, south, viscosity, spin):
    width = centre.shape[-1]
    level = lax.broadcasted_iota(jnp.int32, centre.shape, 1)
    ahead = pltpu.roll(centre, width - 1, axis=2)
    behind = pltpu.roll(centre, 1, axis=2)
    above = jnp.where(level == 7, centre, pltpu.roll(centre, 7, axis=1))
    below = jnp.where(level == 0, centre, pltpu.roll(centre, 1, axis=1))
    spread = viscosity * (north + south + ahead + behind + above + below - 6.0 * centre)
    radial_grad = 0.5 * (north - south)
    azimuth_grad = 0.5 * (ahead - behind)
    rate_density = spread[0] - radial_grad[1] - azimuth_grad[2]
    rate_radial = spread[1] - radial_grad[0] + 2.0 * spin * centre[2]
    rate_azimuth = spread[2] - azimuth_grad[0] - 0.5 * spin * centre[1]
    return jnp.stack([rate_density, rate_radial, rate_azimuth])


def kernel(
    bands, sectors, chunks,
    fields_in, viscosity_in, rotation_in, shifts_in, out,
    fields, viscosity, rotation, shifts, fetched, own, side, first, second, final, partner, lefts, rights, merged, pack, from_ahead, from_behind,
    halo_sent, halo_got, pair_sent, pair_got, right_sent, right_got, left_sent, left_got,
):
    radii = viscosity.shape[0]
    places = sectors // 2
    band = lax.axis_index("rad")
    sector = lax.axis_index("azi")
    place, parity = sector // 2, sector % 2
    has_up, has_down = band < bands - 1, band > 0

    def at(dr, da):
        return (lax.rem(band + dr + bands, bands), lax.rem(sector + da + sectors, sectors))

    barrier = pltpu.get_barrier_semaphore()
    greeted = [(dr, da) for dr in (-1, 0, 1) for da in (-1, 0, 1) if (dr, da) != (0, 0)]
    greeted += [(0, 2 * d - sectors) for d in range(1, places)]
    for dr, da in greeted:
        pl.semaphore_signal(barrier, inc=1, device_id=at(dr, da), device_id_type=MESH)

    fetches = [
        pltpu.make_async_copy(src, dst, fetched.at[i])
        for i, (src, dst) in enumerate(
            [(fields_in, fields), (viscosity_in, viscosity), (rotation_in, rotation), (shifts_in, shifts)]
        )
    ]
    for fetch in fetches:
        fetch.start()
    for fetch in fetches:
        fetch.wait()

    lane = lax.broadcasted_iota(jnp.int32, (8, 128), 1)
    slot = ((lane + 4) // 8) % 16
    for group in range(2):
        packed = None
        for r in range(4 * group, 4 * group + 4):
            for f in range(4):
                if f < 3:
                    tile = fields[f, pl.ds(r, 8, stride=8), :]
                else:
                    tile = jnp.broadcast_to(viscosity[pl.ds(r, 1), :], (8, 128))
                own[DEPTH + r, f] = tile
                index = (r % 4) * 4 + f
                if index == 0:
                    packed = tile
                else:
                    packed = jnp.where(slot == index, pltpu.roll(tile, 8 * index, axis=1), packed)
        pack[group] = packed

    pl.semaphore_wait(barrier, len(greeted))

    def remote(src, dst, sent, got, device):
        return pltpu.make_async_remote_copy(
            src_ref=src, dst_ref=dst, send_sem=sent, recv_sem=got, device_id=device, device_id_type=MESH
        )

    def halo(index, src, dst, device):
        return remote(src, dst, halo_sent.at[index], halo_got.at[index], device)

    last = DEPTH + radii
    up = [
        halo(0, own.at[radii:last], own.at[0:DEPTH], at(1, 0)),
        halo(4, pack.at[1], from_behind.at[0, 1], at(1, 1)),
        halo(5, pack.at[1], from_ahead.at[0, 1], at(1, -1)),
    ]
    down = [
        halo(1, own.at[DEPTH:2 * DEPTH], own.at[last:last + DEPTH], at(-1, 0)),
        halo(6, pack.at[0], from_behind.at[2, 0], at(-1, 1)),
        halo(7, pack.at[0], from_ahead.at[2, 0], at(-1, -1)),
    ]
    across = [
        halo(2, pack, from_behind.at[1], at(0, 1)),
        halo(3, pack, from_ahead.at[1], at(0, -1)),
    ]
    for copy in across:
        copy.start()

    @pl.when(has_up)
    def _():
        for copy in up:
            copy.start()

    @pl.when(has_down)
    def _():
        for copy in down:
            copy.start()

    low = (lane % 8) < 4

    def unpack(dr, group, rows, shift):
        joined = jnp.where(low, from_ahead[dr, group], from_behind[dr, group])
        for r in rows:
            for f in range(4):
                index = (r % 4) * 4 + f
                side[shift + r, f] = joined if index == 0 else pltpu.roll(joined, 128 - 8 * index, axis=1)

    for copy in across:
        copy.wait_recv()
    unpack(1, 0, range(0, 4), DEPTH)
    unpack(1, 1, range(4, 8), DEPTH)

    @pl.when(has_down)
    def _():
        for copy in up:
            copy.wait_recv()
        unpack(0, 1, range(radii - DEPTH, radii), DEPTH - radii)

    @pl.when(jnp.logical_not(has_down))
    def _():
        own[0:DEPTH] = jnp.zeros((DEPTH, 4, 8, 128), jnp.float32)
        side[0:DEPTH] = jnp.zeros((DEPTH, 4, 8, 128), jnp.float32)

    @pl.when(has_up)
    def _():
        for copy in down:
            copy.wait_recv()
        unpack(2, 0, range(0, DEPTH), last)

    @pl.when(jnp.logical_not(has_up))
    def _():
        own[last:last + DEPTH] = jnp.zeros((DEPTH, 4, 8, 128), jnp.float32)
        side[last:last + DEPTH] = jnp.zeros((DEPTH, 4, 8, 128), jnp.float32)

    def start_row(i):
        return jnp.concatenate([own[i, 0:3], side[i, 0:3]], axis=2)

    def row_facts(i):
        row = band * radii + i - DEPTH
        inside = jnp.logical_and(row >= 0, row < bands * radii)
        spin = rotation[jnp.clip(row, 0, bands * radii - 1)]
        return inside, spin, jnp.concatenate([own[i, 3], side[i, 3]], axis=1)

    def first_row(i, _):
        inside, spin, thick = row_facts(i)
        centre = start_row(i)
        rate = neighbour_rates(centre, start_row(i + 1), start_row(i - 1), thick, spin)
        first[i] = jnp.where(inside, centre + time_step * rate, 0.0)
        return 0

    lax.fori_loop(1, radii + 2 * DEPTH - 1, first_row, 0, unroll=True)

    def second_row(i, _):
        inside, spin, thick = row_facts(i)
        centre = first[i]
        rate = neighbour_rates(centre, first[i + 1], first[i - 1], thick, spin)
        second[i] = jnp.where(inside, 0.75 * start_row(i) + 0.25 * (centre + time_step * rate), 0.0)
        return 0

    lax.fori_loop(2, radii + 2 * DEPTH - 2, second_row, 0, unroll=True)

    def final_row(r, _):
        i = r + DEPTH
        inside, spin, thick = row_facts(i)
        centre = second[i]
        rate = neighbour_rates(centre, second[i + 1], second[i - 1], thick, spin)
        final[r] = own[i, 0:3] / 3.0 + 2.0 / 3.0 * (centre + time_step * rate)[..., :128]
        return 0

    per = radii // chunks

    def rows_of(c):
        return pl.ds(c * per, per)

    def pair_copy(c):
        mate = (band, sector + 1 - 2 * parity)
        return remote(final.at[rows_of(c)], partner.at[rows_of(c)], pair_sent.at[c], pair_got.at[c], mate)

    for c in range(chunks):
        lax.fori_loop(c * per, (c + 1) * per, final_row, 0, unroll=True)
        pair_copy(c).start()

    half = lax.broadcasted_iota(jnp.int32, (3, 8, 128), 2) < BLOCK

    def join_row(r):
        shift = shifts[0, band * radii + r]
        here, there = final[r], partner[r]
        left_own = (2 * parity - shift + 2 * sectors) % 4 // 2 == parity
        right_own = (2 * parity + 1 - shift + 2 * sectors) % 4 // 2 == parity
        odd = shift % 2 == 1
        here = jnp.where(odd, pltpu.roll(here, BLOCK, axis=2), here)
        there = jnp.where(odd, pltpu.roll(there, BLOCK, axis=2), there)
        take = jnp.where(half, left_own.astype(jnp.int32), right_own.astype(jnp.int32))
        joined = jnp.where(take == 1, here, there)
        lefts[r // per][place, r % per] = joined
        rights[r // per][place, r % per] = joined

    def line_copy(to_right, d, c):
        if to_right:
            held = lefts[c].at[place]
            return remote(held, held, right_sent.at[d, c], right_got.at[d, c], at(0, 2 * d))
        held = rights[c].at[place]
        return remote(held, held, left_sent.at[d, c], left_got.at[d, c], at(0, -2 * d))

    def end_copy(to_right, c):
        if to_right:
            return remote(merged.at[0, c], lefts[c].at[place], right_sent.at[0, c], right_got.at[0, c], at(0, 2))
        return remote(merged.at[1, c], rights[c].at[place], left_sent.at[0, c], left_got.at[0, c], at(0, -2))

    def ends(to_right):
        return place == places - 2 if to_right else place == 1

    def sends(to_right, d):
        return place + d <= places - 2 if to_right else place - d >= 1

    def gets(to_right, d):
        inner = jnp.logical_and(place >= 1, place <= places - 2)
        return jnp.logical_and(inner, place - d >= 0 if to_right else place + d <= places - 1)

    def gets_end(to_right):
        return place == places - 1 if to_right else place == 0

    def send(c):
        for d in range(places - 2, 0, -1):
            for to_right in (True, False):
                @pl.when(sends(to_right, d))
                def _():
                    line_copy(to_right, d, c).start()

    def get(c):
        for d in range(1, places - 1):
            for to_right in (True, False):
                @pl.when(gets(to_right, d))
                def _():
                    line_copy(to_right, d, c).wait_recv()

    def sources(r, target):
        shift = shifts[0, band * radii + r]
        total = 2 * sectors
        return [(2 * target + h - shift + total) % total // 4 for h in range(2)]

    def send_end(c):
        for to_right in (True, False):
            @pl.when(ends(to_right))
            def _():
                for r in range(c * per, (c + 1) * per):
                    target = sector + 2 if to_right else sector - 2
                    first_from, second_from = sources(r, target)
                    if to_right:
                        pick = lambda at_place: lefts[c][jnp.minimum(at_place, place), r % per]
                    else:
                        pick = lambda at_place: rights[c][jnp.maximum(at_place, place), r % per]
                    merged[1 - int(to_right), c, r % per] = jnp.where(half, pick(first_from), pick(second_from))
                end_copy(to_right, c).start()

    for c in range(chunks):
        pair_copy(c).wait_recv()
        for r in range(c * per, (c + 1) * per):
            join_row(r)
        send(c)

    for c in range(chunks):
        get(c)
        send_end(c)

    for c in range(chunks):
        for to_right in (True, False):
            @pl.when(gets_end(to_right))
            def _():
                end_copy(to_right, c).wait_recv()
        for r in range(c * per, (c + 1) * per):
            def pick(at_place):
                near = jnp.where(place == places - 1, places - 2, at_place)
                left = jnp.where(at_place >= place, place, near)
                far = jnp.where(place == 0, 1, at_place)
                right = jnp.where(at_place <= place, place, far)
                return jnp.where(at_place <= place, lefts[c][left, r % per], rights[c][right, r % per])

            first_from, second_from = sources(r, sector)
            moved = jnp.where(half, pick(first_from), pick(second_from))
            for f in range(3):
                out[f, pl.ds(r, 8, stride=8), :] = moved[f]

    for copy in across:
        copy.wait_send()

    @pl.when(has_up)
    def _():
        for copy in up:
            copy.wait_send()

    @pl.when(has_down)
    def _():
        for copy in down:
            copy.wait_send()

    for c in range(chunks):
        pair_copy(c).wait_send()

    for c in range(chunks):
        for to_right in (True, False):
            @pl.when(ends(to_right))
            def _():
                end_copy(to_right, c).wait_send()

    for d in range(1, places - 1):
        for c in range(chunks):
            for to_right in (True, False):
                @pl.when(sends(to_right, d))
                def _():
                    line_copy(to_right, d, c).wait_send()


def body(fields, viscosity, rotation, shift_blocks):
    bands, sectors = lax.axis_size("rad"), lax.axis_size("azi")
    kinds, height, radii, width = fields.shape
    places, chunks = sectors // 2, 4
    rows = radii + 2 * DEPTH
    steps = places - 1
    vmem = lambda *shape: pltpu.VMEM(shape, jnp.float32)
    dma = lambda *shape: pltpu.SemaphoreType.DMA(shape)
    moved = pl.pallas_call(
        functools.partial(kernel, bands, sectors, chunks),
        out_shape=pltpu.VMEM((kinds, height * radii, width), jnp.float32),
        in_specs=[pl.BlockSpec(memory_space=pltpu.HBM)] * 4,
        out_specs=pl.BlockSpec(memory_space=pltpu.VMEM),
        scratch_shapes=[
            vmem(kinds, height * radii, width), vmem(radii, width),
            pltpu.SMEM(rotation.shape, jnp.float32), pltpu.SMEM(shift_blocks.shape, jnp.int32), dma(4),
            vmem(rows, 4, 8, 128), vmem(rows, 4, 8, 128),
            vmem(rows, 3, 8, 256), vmem(rows, 3, 8, 256),
            vmem(radii, 3, 8, 128), vmem(radii, 3, 8, 128),
            [vmem(places, radii // chunks, 3, 8, 128) for _ in range(chunks)],
            [vmem(places, radii // chunks, 3, 8, 128) for _ in range(chunks)],
            vmem(2, chunks, radii // chunks, 3, 8, 128),
            vmem(2, 8, 128), vmem(3, 2, 8, 128), vmem(3, 2, 8, 128),
            dma(8), dma(8), dma(chunks), dma(chunks),
            dma(steps, chunks), dma(steps, chunks), dma(steps, chunks), dma(steps, chunks),
        ],
        compiler_params=pltpu.CompilerParams(collective_id=0, has_side_effects=True, vmem_limit_bytes=56 * 2**20),
        name="disc_step",
    )(fields.reshape(kinds, height * radii, width), viscosity, rotation, shift_blocks)
    return moved.reshape(fields.shape)


def solution(mesh):
    return jax.shard_map(
        body,
        mesh=mesh,
        in_specs=(P(None, None, "rad", "azi"), P("rad", "azi"), P(), P()),
        out_specs=P(None, None, "rad", "azi"),
        check_vma=False,
    )
```

```python
import functools

import jax
import jax.numpy as jnp
from jax import lax
from jax.experimental import pallas as pl
from jax.experimental.pallas import tpu as pltpu
from jax.sharding import PartitionSpec as P

BLOCK = 64
time_step = 0.3
MESH = pl.DeviceIdType.MESH
DEPTH = 3


def neighbour_rates(centre, north, south, viscosity, spin):
    width = centre.shape[-1]
    level = lax.broadcasted_iota(jnp.int32, centre.shape, 1)
    ahead = pltpu.roll(centre, width - 1, axis=2)
    behind = pltpu.roll(centre, 1, axis=2)
    above = jnp.where(level == 7, centre, pltpu.roll(centre, 7, axis=1))
    below = jnp.where(level == 0, centre, pltpu.roll(centre, 1, axis=1))
    spread = viscosity * (north + south + ahead + behind + above + below - 6.0 * centre)
    radial_grad = 0.5 * (north - south)
    azimuth_grad = 0.5 * (ahead - behind)
    rate_density = spread[0] - radial_grad[1] - azimuth_grad[2]
    rate_radial = spread[1] - radial_grad[0] + 2.0 * spin * centre[2]
    rate_azimuth = spread[2] - azimuth_grad[0] - 0.5 * spin * centre[1]
    return jnp.stack([rate_density, rate_radial, rate_azimuth])


def kernel(
    bands, sectors, chunks,
    fields_in, viscosity_in, rotation_in, shifts_in, out,
    fields, viscosity, rotation, shifts, fetched, own, side, first, second, final, partner, lefts, rights, merged, pack, from_ahead, from_behind,
    halo_sent, halo_got, pair_sent, pair_got, right_sent, right_got, left_sent, left_got,
):
    radii = viscosity.shape[0]
    places = sectors // 2
    band = lax.axis_index("rad")
    sector = lax.axis_index("azi")
    place, parity = sector // 2, sector % 2
    has_up, has_down = band < bands - 1, band > 0

    def at(dr, da):
        return (lax.rem(band + dr + bands, bands), lax.rem(sector + da + sectors, sectors))

    barrier = pltpu.get_barrier_semaphore()
    greeted = [(dr, da) for dr in (-1, 0, 1) for da in (-1, 0, 1) if (dr, da) != (0, 0)]
    greeted += [(0, 2 * d - sectors) for d in range(1, places)]
    for dr, da in greeted:
        pl.semaphore_signal(barrier, inc=1, device_id=at(dr, da), device_id_type=MESH)

    fetches = [
        pltpu.make_async_copy(src, dst, fetched.at[i])
        for i, (src, dst) in enumerate(
            [(fields_in, fields), (viscosity_in, viscosity), (rotation_in, rotation), (shifts_in, shifts)]
        )
    ]
    for fetch in fetches:
        fetch.start()
    for fetch in fetches:
        fetch.wait()

    lane = lax.broadcasted_iota(jnp.int32, (8, 128), 1)
    slot = ((lane + 4) // 8) % 16
    for group in range(2):
        packed = None
        for r in range(4 * group, 4 * group + 4):
            for f in range(4):
                if f < 3:
                    tile = fields[f, pl.ds(r, 8, stride=8), :]
                else:
                    tile = jnp.broadcast_to(viscosity[pl.ds(r, 1), :], (8, 128))
                own[DEPTH + r, f] = tile
                index = (r % 4) * 4 + f
                if index == 0:
                    packed = tile
                else:
                    packed = jnp.where(slot == index, pltpu.roll(tile, 8 * index, axis=1), packed)
        pack[group] = packed

    pl.semaphore_wait(barrier, len(greeted))

    def remote(src, dst, sent, got, device):
        return pltpu.make_async_remote_copy(
            src_ref=src, dst_ref=dst, send_sem=sent, recv_sem=got, device_id=device, device_id_type=MESH
        )

    def halo(index, src, dst, device):
        return remote(src, dst, halo_sent.at[index], halo_got.at[index], device)

    last = DEPTH + radii
    up = [
        halo(0, own.at[radii:last], own.at[0:DEPTH], at(1, 0)),
        halo(4, pack.at[1], from_behind.at[0, 1], at(1, 1)),
        halo(5, pack.at[1], from_ahead.at[0, 1], at(1, -1)),
    ]
    down = [
        halo(1, own.at[DEPTH:2 * DEPTH], own.at[last:last + DEPTH], at(-1, 0)),
        halo(6, pack.at[0], from_behind.at[2, 0], at(-1, 1)),
        halo(7, pack.at[0], from_ahead.at[2, 0], at(-1, -1)),
    ]
    across = [
        halo(2, pack, from_behind.at[1], at(0, 1)),
        halo(3, pack, from_ahead.at[1], at(0, -1)),
    ]
    for copy in across:
        copy.start()

    @pl.when(has_up)
    def _():
        for copy in up:
            copy.start()

    @pl.when(has_down)
    def _():
        for copy in down:
            copy.start()

    low = (lane % 8) < 4

    def unpack(dr, group, rows, shift):
        joined = jnp.where(low, from_ahead[dr, group], from_behind[dr, group])
        for r in rows:
            for f in range(4):
                index = (r % 4) * 4 + f
                side[shift + r, f] = joined if index == 0 else pltpu.roll(joined, 128 - 8 * index, axis=1)

    for copy in across:
        copy.wait_recv()
    unpack(1, 0, range(0, 4), DEPTH)
    unpack(1, 1, range(4, 8), DEPTH)

    @pl.when(has_down)
    def _():
        for copy in up:
            copy.wait_recv()
        unpack(0, 1, range(radii - DEPTH, radii), DEPTH - radii)

    @pl.when(jnp.logical_not(has_down))
    def _():
        own[0:DEPTH] = jnp.zeros((DEPTH, 4, 8, 128), jnp.float32)
        side[0:DEPTH] = jnp.zeros((DEPTH, 4, 8, 128), jnp.float32)

    @pl.when(has_up)
    def _():
        for copy in down:
            copy.wait_recv()
        unpack(2, 0, range(0, DEPTH), last)

    @pl.when(jnp.logical_not(has_up))
    def _():
        own[last:last + DEPTH] = jnp.zeros((DEPTH, 4, 8, 128), jnp.float32)
        side[last:last + DEPTH] = jnp.zeros((DEPTH, 4, 8, 128), jnp.float32)

    def start_row(i):
        return jnp.concatenate([own[i, 0:3], side[i, 0:3]], axis=2)

    def row_facts(i):
        row = band * radii + i - DEPTH
        inside = jnp.logical_and(row >= 0, row < bands * radii)
        spin = rotation[jnp.clip(row, 0, bands * radii - 1)]
        return inside, spin, jnp.concatenate([own[i, 3], side[i, 3]], axis=1)

    def first_row(i, _):
        inside, spin, thick = row_facts(i)
        centre = start_row(i)
        rate = neighbour_rates(centre, start_row(i + 1), start_row(i - 1), thick, spin)
        first[i] = jnp.where(inside, centre + time_step * rate, 0.0)
        return 0

    lax.fori_loop(1, radii + 2 * DEPTH - 1, first_row, 0, unroll=True)

    def second_row(i, _):
        inside, spin, thick = row_facts(i)
        centre = first[i]
        rate = neighbour_rates(centre, first[i + 1], first[i - 1], thick, spin)
        second[i] = jnp.where(inside, 0.75 * start_row(i) + 0.25 * (centre + time_step * rate), 0.0)
        return 0

    lax.fori_loop(2, radii + 2 * DEPTH - 2, second_row, 0, unroll=True)

    def final_row(r, _):
        i = r + DEPTH
        inside, spin, thick = row_facts(i)
        centre = second[i]
        rate = neighbour_rates(centre, second[i + 1], second[i - 1], thick, spin)
        final[r] = own[i, 0:3] / 3.0 + 2.0 / 3.0 * (centre + time_step * rate)[..., :128]
        return 0

    per = radii // chunks

    def rows_of(c):
        return pl.ds(c * per, per)

    def pair_copy(c):
        mate = (band, sector + 1 - 2 * parity)
        return remote(final.at[rows_of(c)], partner.at[rows_of(c)], pair_sent.at[c], pair_got.at[c], mate)

    for c in range(chunks):
        lax.fori_loop(c * per, (c + 1) * per, final_row, 0, unroll=True)
        pair_copy(c).start()

    half = lax.broadcasted_iota(jnp.int32, (3, 8, 128), 2) < BLOCK

    def join_row(r):
        shift = shifts[0, band * radii + r]
        here, there = final[r], partner[r]
        left_own = (2 * parity - shift + 2 * sectors) % 4 // 2 == parity
        right_own = (2 * parity + 1 - shift + 2 * sectors) % 4 // 2 == parity
        odd = shift % 2 == 1
        here = jnp.where(odd, pltpu.roll(here, BLOCK, axis=2), here)
        there = jnp.where(odd, pltpu.roll(there, BLOCK, axis=2), there)
        take = jnp.where(half, left_own.astype(jnp.int32), right_own.astype(jnp.int32))
        joined = jnp.where(take == 1, here, there)
        lefts[r // per][place, r % per] = joined
        rights[r // per][place, r % per] = joined

    def line_copy(to_right, d, c):
        if to_right:
            held = lefts[c].at[place]
            return remote(held, held, right_sent.at[d, c], right_got.at[d, c], at(0, 2 * d))
        held = rights[c].at[place]
        return remote(held, held, left_sent.at[d, c], left_got.at[d, c], at(0, -2 * d))

    def end_copy(to_right, c):
        if to_right:
            return remote(merged.at[0, c], lefts[c].at[place], right_sent.at[0, c], right_got.at[0, c], at(0, 2))
        return remote(merged.at[1, c], rights[c].at[place], left_sent.at[0, c], left_got.at[0, c], at(0, -2))

    def ends(to_right):
        return place == places - 2 if to_right else place == 1

    def sends(to_right, d):
        return place + d <= places - 2 if to_right else place - d >= 1

    def gets(to_right, d):
        inner = jnp.logical_and(place >= 1, place <= places - 2)
        return jnp.logical_and(inner, place - d >= 0 if to_right else place + d <= places - 1)

    def gets_end(to_right):
        return place == places - 1 if to_right else place == 0

    def send(c, urgent):
        for d in range(places - 2, 0, -1):
            for to_right in (True, False):
                far = place + d == places - 2 if to_right else place - d == 1
                wanted = far if urgent else jnp.logical_not(far)

                @pl.when(jnp.logical_and(sends(to_right, d), wanted))
                def _():
                    line_copy(to_right, d, c).start()

    def get(c):
        for d in range(1, places - 1):
            for to_right in (True, False):
                @pl.when(gets(to_right, d))
                def _():
                    line_copy(to_right, d, c).wait_recv()

    def sources(r, target):
        shift = shifts[0, band * radii + r]
        total = 2 * sectors
        return [(2 * target + h - shift + total) % total // 4 for h in range(2)]

    def send_end(c):
        for to_right in (True, False):
            @pl.when(ends(to_right))
            def _():
                for r in range(c * per, (c + 1) * per):
                    target = sector + 2 if to_right else sector - 2
                    first_from, second_from = sources(r, target)
                    if to_right:
                        pick = lambda at_place: lefts[c][jnp.minimum(at_place, place), r % per]
                    else:
                        pick = lambda at_place: rights[c][jnp.maximum(at_place, place), r % per]
                    merged[1 - int(to_right), c, r % per] = jnp.where(half, pick(first_from), pick(second_from))
                end_copy(to_right, c).start()

    for c in range(chunks):
        pair_copy(c).wait_recv()
        for r in range(c * per, (c + 1) * per):
            join_row(r)
        send(c, True)

    for c in range(chunks):
        send(c, False)

    for c in range(chunks):
        get(c)
        send_end(c)

    for c in range(chunks):
        for to_right in (True, False):
            @pl.when(gets_end(to_right))
            def _():
                end_copy(to_right, c).wait_recv()
        for r in range(c * per, (c + 1) * per):
            def pick(at_place):
                near = jnp.where(place == places - 1, places - 2, at_place)
                left = jnp.where(at_place >= place, place, near)
                far = jnp.where(place == 0, 1, at_place)
                right = jnp.where(at_place <= place, place, far)
                return jnp.where(at_place <= place, lefts[c][left, r % per], rights[c][right, r % per])

            first_from, second_from = sources(r, sector)
            moved = jnp.where(half, pick(first_from), pick(second_from))
            for f in range(3):
                out[f, pl.ds(r, 8, stride=8), :] = moved[f]

    for copy in across:
        copy.wait_send()

    @pl.when(has_up)
    def _():
        for copy in up:
            copy.wait_send()

    @pl.when(has_down)
    def _():
        for copy in down:
            copy.wait_send()

    for c in range(chunks):
        pair_copy(c).wait_send()

    for c in range(chunks):
        for to_right in (True, False):
            @pl.when(ends(to_right))
            def _():
                end_copy(to_right, c).wait_send()

    for d in range(1, places - 1):
        for c in range(chunks):
            for to_right in (True, False):
                @pl.when(sends(to_right, d))
                def _():
                    line_copy(to_right, d, c).wait_send()


def body(fields, viscosity, rotation, shift_blocks):
    bands, sectors = lax.axis_size("rad"), lax.axis_size("azi")
    kinds, height, radii, width = fields.shape
    places, chunks = sectors // 2, 4
    rows = radii + 2 * DEPTH
    steps = places - 1
    vmem = lambda *shape: pltpu.VMEM(shape, jnp.float32)
    dma = lambda *shape: pltpu.SemaphoreType.DMA(shape)
    moved = pl.pallas_call(
        functools.partial(kernel, bands, sectors, chunks),
        out_shape=pltpu.VMEM((kinds, height * radii, width), jnp.float32),
        in_specs=[pl.BlockSpec(memory_space=pltpu.HBM)] * 4,
        out_specs=pl.BlockSpec(memory_space=pltpu.VMEM),
        scratch_shapes=[
            vmem(kinds, height * radii, width), vmem(radii, width),
            pltpu.SMEM(rotation.shape, jnp.float32), pltpu.SMEM(shift_blocks.shape, jnp.int32), dma(4),
            vmem(rows, 4, 8, 128), vmem(rows, 4, 8, 128),
            vmem(rows, 3, 8, 256), vmem(rows, 3, 8, 256),
            vmem(radii, 3, 8, 128), vmem(radii, 3, 8, 128),
            [vmem(places, radii // chunks, 3, 8, 128) for _ in range(chunks)],
            [vmem(places, radii // chunks, 3, 8, 128) for _ in range(chunks)],
            vmem(2, chunks, radii // chunks, 3, 8, 128),
            vmem(2, 8, 128), vmem(3, 2, 8, 128), vmem(3, 2, 8, 128),
            dma(8), dma(8), dma(chunks), dma(chunks),
            dma(steps, chunks), dma(steps, chunks), dma(steps, chunks), dma(steps, chunks),
        ],
        compiler_params=pltpu.CompilerParams(collective_id=0, has_side_effects=True, vmem_limit_bytes=56 * 2**20),
        name="disc_step",
    )(fields.reshape(kinds, height * radii, width), viscosity, rotation, shift_blocks)
    return moved.reshape(fields.shape)


def solution(mesh):
    return jax.shard_map(
        body,
        mesh=mesh,
        in_specs=(P(None, None, "rad", "azi"), P("rad", "azi"), P(), P()),
        out_specs=P(None, None, "rad", "azi"),
        check_vma=False,
    )
```

```python
import functools

import jax
import jax.numpy as jnp
from jax import lax
from jax.experimental import pallas as pl
from jax.experimental.pallas import tpu as pltpu
from jax.sharding import PartitionSpec as P

BLOCK = 64
time_step = 0.3
MESH = pl.DeviceIdType.MESH
DEPTH = 3


def neighbour_rates(centre, north, south, viscosity, spin):
    width = centre.shape[-1]
    level = lax.broadcasted_iota(jnp.int32, centre.shape, 1)
    ahead = pltpu.roll(centre, width - 1, axis=2)
    behind = pltpu.roll(centre, 1, axis=2)
    above = jnp.where(level == 7, centre, pltpu.roll(centre, 7, axis=1))
    below = jnp.where(level == 0, centre, pltpu.roll(centre, 1, axis=1))
    spread = viscosity * (north + south + ahead + behind + above + below - 6.0 * centre)
    radial_grad = 0.5 * (north - south)
    azimuth_grad = 0.5 * (ahead - behind)
    rate_density = spread[0] - radial_grad[1] - azimuth_grad[2]
    rate_radial = spread[1] - radial_grad[0] + 2.0 * spin * centre[2]
    rate_azimuth = spread[2] - azimuth_grad[0] - 0.5 * spin * centre[1]
    return jnp.stack([rate_density, rate_radial, rate_azimuth])


def kernel(
    bands, sectors, chunks,
    fields_in, viscosity_in, rotation_in, shifts_in, out,
    fields, viscosity, rotation, shifts, fetched, own, side, first, second, final, partner, lefts, rights, merged, pack, from_ahead, from_behind,
    halo_sent, halo_got, pair_sent, pair_got, right_sent, right_got, left_sent, left_got,
):
    radii = viscosity.shape[0]
    places = sectors // 2
    band = lax.axis_index("rad")
    sector = lax.axis_index("azi")
    place, parity = sector // 2, sector % 2
    has_up, has_down = band < bands - 1, band > 0

    def at(dr, da):
        return (lax.rem(band + dr + bands, bands), lax.rem(sector + da + sectors, sectors))

    barrier = pltpu.get_barrier_semaphore()
    greeted = [(dr, da) for dr in (-1, 0, 1) for da in (-1, 0, 1) if (dr, da) != (0, 0)]
    greeted += [(0, 2 * d - sectors) for d in range(1, places)]
    for dr, da in greeted:
        pl.semaphore_signal(barrier, inc=1, device_id=at(dr, da), device_id_type=MESH)

    fetches = [
        pltpu.make_async_copy(src, dst, fetched.at[i])
        for i, (src, dst) in enumerate(
            [(fields_in, fields), (viscosity_in, viscosity), (rotation_in, rotation), (shifts_in, shifts)]
        )
    ]
    for fetch in fetches:
        fetch.start()
    for fetch in fetches:
        fetch.wait()

    lane = lax.broadcasted_iota(jnp.int32, (8, 128), 1)
    slot = ((lane + 4) // 8) % 16
    for group in range(2):
        packed = None
        for r in range(4 * group, 4 * group + 4):
            for f in range(4):
                if f < 3:
                    tile = fields[f, pl.ds(r, 8, stride=8), :]
                else:
                    tile = jnp.broadcast_to(viscosity[pl.ds(r, 1), :], (8, 128))
                own[DEPTH + r, f] = tile
                index = (r % 4) * 4 + f
                if index == 0:
                    packed = tile
                else:
                    packed = jnp.where(slot == index, pltpu.roll(tile, 8 * index, axis=1), packed)
        pack[group] = packed

    pl.semaphore_wait(barrier, len(greeted))

    def remote(src, dst, sent, got, device):
        return pltpu.make_async_remote_copy(
            src_ref=src, dst_ref=dst, send_sem=sent, recv_sem=got, device_id=device, device_id_type=MESH
        )

    def halo(index, src, dst, device):
        return remote(src, dst, halo_sent.at[index], halo_got.at[index], device)

    last = DEPTH + radii
    up = [
        halo(0, own.at[radii:last], own.at[0:DEPTH], at(1, 0)),
        halo(4, pack.at[1], from_behind.at[0, 1], at(1, 1)),
        halo(5, pack.at[1], from_ahead.at[0, 1], at(1, -1)),
    ]
    down = [
        halo(1, own.at[DEPTH:2 * DEPTH], own.at[last:last + DEPTH], at(-1, 0)),
        halo(6, pack.at[0], from_behind.at[2, 0], at(-1, 1)),
        halo(7, pack.at[0], from_ahead.at[2, 0], at(-1, -1)),
    ]
    across = [
        halo(2, pack, from_behind.at[1], at(0, 1)),
        halo(3, pack, from_ahead.at[1], at(0, -1)),
    ]
    for copy in across:
        copy.start()

    @pl.when(has_up)
    def _():
        for copy in up:
            copy.start()

    @pl.when(has_down)
    def _():
        for copy in down:
            copy.start()

    low = (lane % 8) < 4

    def unpack(dr, group, rows, shift):
        joined = jnp.where(low, from_ahead[dr, group], from_behind[dr, group])
        for r in rows:
            for f in range(4):
                index = (r % 4) * 4 + f
                side[shift + r, f] = joined if index == 0 else pltpu.roll(joined, 128 - 8 * index, axis=1)

    for copy in across:
        copy.wait_recv()
    unpack(1, 0, range(0, 4), DEPTH)
    unpack(1, 1, range(4, 8), DEPTH)

    @pl.when(has_down)
    def _():
        for copy in up:
            copy.wait_recv()
        unpack(0, 1, range(radii - DEPTH, radii), DEPTH - radii)

    @pl.when(jnp.logical_not(has_down))
    def _():
        own[0:DEPTH] = jnp.zeros((DEPTH, 4, 8, 128), jnp.float32)
        side[0:DEPTH] = jnp.zeros((DEPTH, 4, 8, 128), jnp.float32)

    @pl.when(has_up)
    def _():
        for copy in down:
            copy.wait_recv()
        unpack(2, 0, range(0, DEPTH), last)

    @pl.when(jnp.logical_not(has_up))
    def _():
        own[last:last + DEPTH] = jnp.zeros((DEPTH, 4, 8, 128), jnp.float32)
        side[last:last + DEPTH] = jnp.zeros((DEPTH, 4, 8, 128), jnp.float32)

    def start_row(i):
        return jnp.concatenate([own[i, 0:3], side[i, 0:3]], axis=2)

    def row_facts(i):
        row = band * radii + i - DEPTH
        inside = jnp.logical_and(row >= 0, row < bands * radii)
        spin = rotation[jnp.clip(row, 0, bands * radii - 1)]
        return inside, spin, jnp.concatenate([own[i, 3], side[i, 3]], axis=1)

    def first_row(i, _):
        inside, spin, thick = row_facts(i)
        centre = start_row(i)
        rate = neighbour_rates(centre, start_row(i + 1), start_row(i - 1), thick, spin)
        first[i] = jnp.where(inside, centre + time_step * rate, 0.0)
        return 0

    lax.fori_loop(1, radii + 2 * DEPTH - 1, first_row, 0, unroll=True)

    def second_row(i, _):
        inside, spin, thick = row_facts(i)
        centre = first[i]
        rate = neighbour_rates(centre, first[i + 1], first[i - 1], thick, spin)
        second[i] = jnp.where(inside, 0.75 * start_row(i) + 0.25 * (centre + time_step * rate), 0.0)
        return 0

    lax.fori_loop(2, radii + 2 * DEPTH - 2, second_row, 0, unroll=True)

    def final_row(r, _):
        i = r + DEPTH
        inside, spin, thick = row_facts(i)
        centre = second[i]
        rate = neighbour_rates(centre, second[i + 1], second[i - 1], thick, spin)
        final[r] = own[i, 0:3] / 3.0 + 2.0 / 3.0 * (centre + time_step * rate)[..., :128]
        return 0

    per = radii // chunks

    def rows_of(c):
        return pl.ds(c * per, per)

    def pair_copy(c):
        mate = (band, sector + 1 - 2 * parity)
        return remote(final.at[rows_of(c)], partner.at[rows_of(c)], pair_sent.at[c], pair_got.at[c], mate)

    for c in range(chunks):
        lax.fori_loop(c * per, (c + 1) * per, final_row, 0, unroll=True)
        pair_copy(c).start()

    half = lax.broadcasted_iota(jnp.int32, (3, 8, 128), 2) < BLOCK

    def join_row(r):
        shift = shifts[0, band * radii + r]
        here, there = final[r], partner[r]
        left_own = (2 * parity - shift + 2 * sectors) % 4 // 2 == parity
        right_own = (2 * parity + 1 - shift + 2 * sectors) % 4 // 2 == parity
        odd = shift % 2 == 1
        here = jnp.where(odd, pltpu.roll(here, BLOCK, axis=2), here)
        there = jnp.where(odd, pltpu.roll(there, BLOCK, axis=2), there)
        take = jnp.where(half, left_own.astype(jnp.int32), right_own.astype(jnp.int32))
        joined = jnp.where(take == 1, here, there)
        lefts[r // per][place, r % per] = joined
        rights[r // per][place, r % per] = joined

    def line_copy(to_right, d, c):
        if to_right:
            held = lefts[c].at[place]
            return remote(held, held, right_sent.at[d, c], right_got.at[d, c], at(0, 2 * d))
        held = rights[c].at[place]
        return remote(held, held, left_sent.at[d, c], left_got.at[d, c], at(0, -2 * d))

    def end_copy(to_right, c):
        if to_right:
            return remote(merged.at[0, c], lefts[c].at[place], right_sent.at[0, c], right_got.at[0, c], at(0, 2))
        return remote(merged.at[1, c], rights[c].at[place], left_sent.at[0, c], left_got.at[0, c], at(0, -2))

    def ends(to_right):
        return place == places - 2 if to_right else place == 1

    def sends(to_right, d):
        return place + d <= places - 2 if to_right else place - d >= 1

    def gets(to_right, d):
        inner = jnp.logical_and(place >= 1, place <= places - 2)
        return jnp.logical_and(inner, place - d >= 0 if to_right else place + d <= places - 1)

    def gets_end(to_right):
        return place == places - 1 if to_right else place == 0

    def send(c, urgent):
        for d in range(places - 2, 0, -1):
            for to_right in (True, False):
                far = place + d == places - 2 if to_right else place - d == 1
                wanted = far if urgent else jnp.logical_not(far)

                @pl.when(jnp.logical_and(sends(to_right, d), wanted))
                def _():
                    line_copy(to_right, d, c).start()

    def get(c, urgent):
        for d in range(1, places - 1):
            for to_right in (True, False):
                wanted = ends(to_right) if urgent else jnp.logical_not(ends(to_right))

                @pl.when(jnp.logical_and(gets(to_right, d), wanted))
                def _():
                    line_copy(to_right, d, c).wait_recv()

    def sources(r, target):
        shift = shifts[0, band * radii + r]
        total = 2 * sectors
        return [(2 * target + h - shift + total) % total // 4 for h in range(2)]

    def send_end(c):
        for to_right in (True, False):
            @pl.when(ends(to_right))
            def _():
                for r in range(c * per, (c + 1) * per):
                    target = sector + 2 if to_right else sector - 2
                    first_from, second_from = sources(r, target)
                    if to_right:
                        pick = lambda at_place: lefts[c][jnp.minimum(at_place, place), r % per]
                    else:
                        pick = lambda at_place: rights[c][jnp.maximum(at_place, place), r % per]
                    merged[1 - int(to_right), c, r % per] = jnp.where(half, pick(first_from), pick(second_from))
                end_copy(to_right, c).start()

    for c in range(chunks):
        pair_copy(c).wait_recv()
        for r in range(c * per, (c + 1) * per):
            join_row(r)
        send(c, True)

    for c in range(chunks):
        send(c, False)

    for c in range(chunks):
        get(c, True)
        send_end(c)

    for c in range(chunks):
        get(c, False)
        for to_right in (True, False):
            @pl.when(gets_end(to_right))
            def _():
                end_copy(to_right, c).wait_recv()
        for r in range(c * per, (c + 1) * per):
            def pick(at_place):
                near = jnp.where(place == places - 1, places - 2, at_place)
                left = jnp.where(at_place >= place, place, near)
                far = jnp.where(place == 0, 1, at_place)
                right = jnp.where(at_place <= place, place, far)
                return jnp.where(at_place <= place, lefts[c][left, r % per], rights[c][right, r % per])

            first_from, second_from = sources(r, sector)
            moved = jnp.where(half, pick(first_from), pick(second_from))
            for f in range(3):
                out[f, pl.ds(r, 8, stride=8), :] = moved[f]

    for copy in across:
        copy.wait_send()

    @pl.when(has_up)
    def _():
        for copy in up:
            copy.wait_send()

    @pl.when(has_down)
    def _():
        for copy in down:
            copy.wait_send()

    for c in range(chunks):
        pair_copy(c).wait_send()

    for c in range(chunks):
        for to_right in (True, False):
            @pl.when(ends(to_right))
            def _():
                end_copy(to_right, c).wait_send()

    for d in range(1, places - 1):
        for c in range(chunks):
            for to_right in (True, False):
                @pl.when(sends(to_right, d))
                def _():
                    line_copy(to_right, d, c).wait_send()


def body(fields, viscosity, rotation, shift_blocks):
    bands, sectors = lax.axis_size("rad"), lax.axis_size("azi")
    kinds, height, radii, width = fields.shape
    places, chunks = sectors // 2, 4
    rows = radii + 2 * DEPTH
    steps = places - 1
    vmem = lambda *shape: pltpu.VMEM(shape, jnp.float32)
    dma = lambda *shape: pltpu.SemaphoreType.DMA(shape)
    moved = pl.pallas_call(
        functools.partial(kernel, bands, sectors, chunks),
        out_shape=pltpu.VMEM((kinds, height * radii, width), jnp.float32),
        in_specs=[pl.BlockSpec(memory_space=pltpu.HBM)] * 4,
        out_specs=pl.BlockSpec(memory_space=pltpu.VMEM),
        scratch_shapes=[
            vmem(kinds, height * radii, width), vmem(radii, width),
            pltpu.SMEM(rotation.shape, jnp.float32), pltpu.SMEM(shift_blocks.shape, jnp.int32), dma(4),
            vmem(rows, 4, 8, 128), vmem(rows, 4, 8, 128),
            vmem(rows, 3, 8, 256), vmem(rows, 3, 8, 256),
            vmem(radii, 3, 8, 128), vmem(radii, 3, 8, 128),
            [vmem(places, radii // chunks, 3, 8, 128) for _ in range(chunks)],
            [vmem(places, radii // chunks, 3, 8, 128) for _ in range(chunks)],
            vmem(2, chunks, radii // chunks, 3, 8, 128),
            vmem(2, 8, 128), vmem(3, 2, 8, 128), vmem(3, 2, 8, 128),
            dma(8), dma(8), dma(chunks), dma(chunks),
            dma(steps, chunks), dma(steps, chunks), dma(steps, chunks), dma(steps, chunks),
        ],
        compiler_params=pltpu.CompilerParams(collective_id=0, has_side_effects=True, vmem_limit_bytes=56 * 2**20),
        name="disc_step",
    )(fields.reshape(kinds, height * radii, width), viscosity, rotation, shift_blocks)
    return moved.reshape(fields.shape)


def solution(mesh):
    return jax.shard_map(
        body,
        mesh=mesh,
        in_specs=(P(None, None, "rad", "azi"), P("rad", "azi"), P(), P()),
        out_specs=P(None, None, "rad", "azi"),
        check_vma=False,
    )
```

```python
import functools

import jax
import jax.numpy as jnp
from jax import lax
from jax.experimental import pallas as pl
from jax.experimental.pallas import tpu as pltpu
from jax.sharding import PartitionSpec as P

BLOCK = 64
time_step = 0.3
MESH = pl.DeviceIdType.MESH
DEPTH = 3


def neighbour_rates(centre, north, south, viscosity, spin):
    width = centre.shape[-1]
    level = lax.broadcasted_iota(jnp.int32, centre.shape, 1)
    ahead = pltpu.roll(centre, width - 1, axis=2)
    behind = pltpu.roll(centre, 1, axis=2)
    above = jnp.where(level == 7, centre, pltpu.roll(centre, 7, axis=1))
    below = jnp.where(level == 0, centre, pltpu.roll(centre, 1, axis=1))
    spread = viscosity * (north + south + ahead + behind + above + below - 6.0 * centre)
    radial_grad = 0.5 * (north - south)
    azimuth_grad = 0.5 * (ahead - behind)
    rate_density = spread[0] - radial_grad[1] - azimuth_grad[2]
    rate_radial = spread[1] - radial_grad[0] + 2.0 * spin * centre[2]
    rate_azimuth = spread[2] - azimuth_grad[0] - 0.5 * spin * centre[1]
    return jnp.stack([rate_density, rate_radial, rate_azimuth])


def kernel(
    bands, sectors, chunks,
    fields_in, viscosity_in, rotation_in, shifts_in, out,
    fields, viscosity, rotation, shifts, fetched, own, side, first, second, raws, gots, staged, pack, from_ahead, from_behind,
    halo_sent, halo_got, mate_sent, mate_got, end_sent, end_got, right_sent, right_got, left_sent, left_got,
):
    radii = viscosity.shape[0]
    places = sectors // 2
    band = lax.axis_index("rad")
    sector = lax.axis_index("azi")
    place, parity = sector // 2, sector % 2
    has_up, has_down = band < bands - 1, band > 0

    def at(dr, da):
        return (lax.rem(band + dr + bands, bands), lax.rem(sector + da + sectors, sectors))

    barrier = pltpu.get_barrier_semaphore()
    greeted = [(dr, da) for dr in (-1, 0, 1) for da in (-1, 0, 1) if (dr, da) != (0, 0)]
    greeted += [(0, 2 * d - sectors) for d in range(1, places)] + [(0, -3), (0, 3)]
    for dr, da in greeted:
        pl.semaphore_signal(barrier, inc=1, device_id=at(dr, da), device_id_type=MESH)

    fetches = [
        pltpu.make_async_copy(src, dst, fetched.at[i])
        for i, (src, dst) in enumerate(
            [(fields_in, fields), (viscosity_in, viscosity), (rotation_in, rotation), (shifts_in, shifts)]
        )
    ]
    for fetch in fetches:
        fetch.start()
    for fetch in fetches:
        fetch.wait()

    lane = lax.broadcasted_iota(jnp.int32, (8, 128), 1)
    slot = ((lane + 4) // 8) % 16
    for group in range(2):
        packed = None
        for r in range(4 * group, 4 * group + 4):
            for f in range(4):
                if f < 3:
                    tile = fields[f, pl.ds(r, 8, stride=8), :]
                else:
                    tile = jnp.broadcast_to(viscosity[pl.ds(r, 1), :], (8, 128))
                own[DEPTH + r, f] = tile
                index = (r % 4) * 4 + f
                if index == 0:
                    packed = tile
                else:
                    packed = jnp.where(slot == index, pltpu.roll(tile, 8 * index, axis=1), packed)
        pack[group] = packed

    pl.semaphore_wait(barrier, len(greeted))

    def remote(src, dst, sent, got, device):
        return pltpu.make_async_remote_copy(
            src_ref=src, dst_ref=dst, send_sem=sent, recv_sem=got, device_id=device, device_id_type=MESH
        )

    def halo(index, src, dst, device):
        return remote(src, dst, halo_sent.at[index], halo_got.at[index], device)

    last = DEPTH + radii
    up = [
        halo(0, own.at[radii:last], own.at[0:DEPTH], at(1, 0)),
        halo(4, pack.at[1], from_behind.at[0, 1], at(1, 1)),
        halo(5, pack.at[1], from_ahead.at[0, 1], at(1, -1)),
    ]
    down = [
        halo(1, own.at[DEPTH:2 * DEPTH], own.at[last:last + DEPTH], at(-1, 0)),
        halo(6, pack.at[0], from_behind.at[2, 0], at(-1, 1)),
        halo(7, pack.at[0], from_ahead.at[2, 0], at(-1, -1)),
    ]
    across = [
        halo(2, pack, from_behind.at[1], at(0, 1)),
        halo(3, pack, from_ahead.at[1], at(0, -1)),
    ]
    for copy in across:
        copy.start()

    @pl.when(has_up)
    def _():
        for copy in up:
            copy.start()

    @pl.when(has_down)
    def _():
        for copy in down:
            copy.start()

    low = (lane % 8) < 4

    def unpack(dr, group, rows, shift):
        joined = jnp.where(low, from_ahead[dr, group], from_behind[dr, group])
        for r in rows:
            for f in range(4):
                index = (r % 4) * 4 + f
                side[shift + r, f] = joined if index == 0 else pltpu.roll(joined, 128 - 8 * index, axis=1)

    for copy in across:
        copy.wait_recv()
    unpack(1, 0, range(0, 4), DEPTH)
    unpack(1, 1, range(4, 8), DEPTH)

    @pl.when(has_down)
    def _():
        for copy in up:
            copy.wait_recv()
        unpack(0, 1, range(radii - DEPTH, radii), DEPTH - radii)

    @pl.when(jnp.logical_not(has_down))
    def _():
        own[0:DEPTH] = jnp.zeros((DEPTH, 4, 8, 128), jnp.float32)
        side[0:DEPTH] = jnp.zeros((DEPTH, 4, 8, 128), jnp.float32)

    @pl.when(has_up)
    def _():
        for copy in down:
            copy.wait_recv()
        unpack(2, 0, range(0, DEPTH), last)

    @pl.when(jnp.logical_not(has_up))
    def _():
        own[last:last + DEPTH] = jnp.zeros((DEPTH, 4, 8, 128), jnp.float32)
        side[last:last + DEPTH] = jnp.zeros((DEPTH, 4, 8, 128), jnp.float32)

    def start_row(i):
        return jnp.concatenate([own[i, 0:3], side[i, 0:3]], axis=2)

    def row_facts(i):
        row = band * radii + i - DEPTH
        inside = jnp.logical_and(row >= 0, row < bands * radii)
        spin = rotation[jnp.clip(row, 0, bands * radii - 1)]
        return inside, spin, jnp.concatenate([own[i, 3], side[i, 3]], axis=1)

    def first_row(i, _):
        inside, spin, thick = row_facts(i)
        centre = start_row(i)
        rate = neighbour_rates(centre, start_row(i + 1), start_row(i - 1), thick, spin)
        first[i] = jnp.where(inside, centre + time_step * rate, 0.0)
        return 0

    lax.fori_loop(1, radii + 2 * DEPTH - 1, first_row, 0, unroll=True)

    def second_row(i, _):
        inside, spin, thick = row_facts(i)
        centre = first[i]
        rate = neighbour_rates(centre, first[i + 1], first[i - 1], thick, spin)
        second[i] = jnp.where(inside, 0.75 * start_row(i) + 0.25 * (centre + time_step * rate), 0.0)
        return 0

    lax.fori_loop(2, radii + 2 * DEPTH - 2, second_row, 0, unroll=True)

    per = radii // chunks

    def final_row(c, r):
        i = r + DEPTH
        inside, spin, thick = row_facts(i)
        centre = second[i]
        rate = neighbour_rates(centre, second[i + 1], second[i - 1], thick, spin)
        raws[c][place, r - c * per] = own[i, 0:3] / 3.0 + 2.0 / 3.0 * (centre + time_step * rate)[..., :128]

    def line_copy(to_right, d, c):
        held = raws[c].at[place]
        if to_right:
            return remote(held, held, right_sent.at[d, c], right_got.at[d, c], at(0, 2 * d))
        return remote(held, held, left_sent.at[d, c], left_got.at[d, c], at(0, -2 * d))

    def sends(to_right, d):
        return place + d <= places - 2 if to_right else place - d >= 1

    def gets(to_right, d):
        inner = jnp.logical_and(place >= 1, place <= places - 2)
        return jnp.logical_and(inner, place - d >= 0 if to_right else place + d <= places - 1)

    def send(c):
        for d in range(places - 2, 0, -1):
            for to_right in (True, False):
                @pl.when(sends(to_right, d))
                def _():
                    line_copy(to_right, d, c).start()

    def get(c):
        for d in range(1, places - 1):
            for to_right in (True, False):
                @pl.when(gets(to_right, d))
                def _():
                    line_copy(to_right, d, c).wait_recv()

    for c in range(chunks):
        for r in range(c * per, (c + 1) * per):
            final_row(c, r)
        send(c)

    half = lax.broadcasted_iota(jnp.int32, (3, 8, 128), 2) < BLOCK
    total = 2 * sectors

    def sources(r, target):
        shift = shifts[0, band * radii + r]
        to_first = (2 * target - shift + total) % total // 2
        to_second = (2 * target + 1 - shift + total) % total // 2
        odd = shift % 2 == 1
        return jnp.where(odd, to_second, to_first), jnp.where(odd, to_first, to_second), odd

    def picked(c, r, target):
        low_from, high_from, _ = sources(r, target)
        return jnp.where(half, raws[c][low_from // 2, r - c * per], raws[c][high_from // 2, r - c * per])

    inner = jnp.logical_and(place >= 1, place <= places - 2)
    outer = jnp.logical_not(inner)
    beside = jnp.logical_or(place == 1, place == places - 2)
    mate = sector + 1 - 2 * parity
    end = sector + jnp.where(place == 1, -2, 2)
    end_mate = end + 1 - 2 * parity

    def mate_copy(c):
        return remote(staged.at[0, c], gots[c].at[parity], mate_sent.at[c], mate_got.at[c], (band, mate))

    def end_copy(other, c):
        target = lax.rem((end_mate if other else end) + sectors, sectors)
        return remote(
            staged.at[1 + other, c], gots[c].at[parity], end_sent.at[other, c], end_got.at[parity, c], (band, target)
        )

    def from_helper(q, c):
        return remote(gots[c].at[q], gots[c].at[q], end_sent.at[q, c], end_got.at[q, c], (band, mate))

    for c in range(chunks):
        get(c)
        rows = range(c * per, (c + 1) * per)

        @pl.when(beside)
        def _():
            for other, target in ((0, end), (1, end_mate)):
                for r in rows:
                    staged[1 + other, c, r - c * per] = picked(c, r, target)
                end_copy(other, c).start()

        @pl.when(inner)
        def _():
            for r in rows:
                staged[0, c, r - c * per] = picked(c, r, mate)
            mate_copy(c).start()
            for r in rows:
                gots[c][parity, r - c * per] = picked(c, r, sector)

    for c in range(chunks):
        @pl.when(inner)
        def _():
            mate_copy(c).wait_recv()

        @pl.when(outer)
        def _():
            for q in range(2):
                from_helper(q, c).wait_recv()

        for r in range(c * per, (c + 1) * per):
            low_from, high_from, odd = sources(r, sector)
            moved = jnp.where(half, gots[c][low_from % 2, r - c * per], gots[c][high_from % 2, r - c * per])
            moved = jnp.where(odd, pltpu.roll(moved, BLOCK, axis=2), moved)
            for f in range(3):
                out[f, pl.ds(r, 8, stride=8), :] = moved[f]

    for copy in across:
        copy.wait_send()

    @pl.when(has_up)
    def _():
        for copy in up:
            copy.wait_send()

    @pl.when(has_down)
    def _():
        for copy in down:
            copy.wait_send()

    for c in range(chunks):
        @pl.when(beside)
        def _():
            for other in range(2):
                end_copy(other, c).wait_send()

        @pl.when(inner)
        def _():
            mate_copy(c).wait_send()

    for d in range(1, places - 1):
        for c in range(chunks):
            for to_right in (True, False):
                @pl.when(sends(to_right, d))
                def _():
                    line_copy(to_right, d, c).wait_send()


def body(fields, viscosity, rotation, shift_blocks):
    bands, sectors = lax.axis_size("rad"), lax.axis_size("azi")
    kinds, height, radii, width = fields.shape
    places, chunks = sectors // 2, 4
    rows = radii + 2 * DEPTH
    steps = places - 1
    vmem = lambda *shape: pltpu.VMEM(shape, jnp.float32)
    dma = lambda *shape: pltpu.SemaphoreType.DMA(shape)
    moved = pl.pallas_call(
        functools.partial(kernel, bands, sectors, chunks),
        out_shape=pltpu.VMEM((kinds, height * radii, width), jnp.float32),
        in_specs=[pl.BlockSpec(memory_space=pltpu.HBM)] * 4,
        out_specs=pl.BlockSpec(memory_space=pltpu.VMEM),
        scratch_shapes=[
            vmem(kinds, height * radii, width), vmem(radii, width),
            pltpu.SMEM(rotation.shape, jnp.float32), pltpu.SMEM(shift_blocks.shape, jnp.int32), dma(4),
            vmem(rows, 4, 8, 128), vmem(rows, 4, 8, 128),
            vmem(rows, 3, 8, 256), vmem(rows, 3, 8, 256),
            [vmem(places, radii // chunks, 3, 8, 128) for _ in range(chunks)],
            [vmem(2, radii // chunks, 3, 8, 128) for _ in range(chunks)],
            vmem(3, chunks, radii // chunks, 3, 8, 128),
            vmem(2, 8, 128), vmem(3, 2, 8, 128), vmem(3, 2, 8, 128),
            dma(8), dma(8), dma(chunks), dma(chunks), dma(2, chunks), dma(2, chunks),
            dma(steps, chunks), dma(steps, chunks), dma(steps, chunks), dma(steps, chunks),
        ],
        compiler_params=pltpu.CompilerParams(collective_id=0, has_side_effects=True, vmem_limit_bytes=56 * 2**20),
        name="disc_step",
    )(fields.reshape(kinds, height * radii, width), viscosity, rotation, shift_blocks)
    return moved.reshape(fields.shape)


def solution(mesh):
    return jax.shard_map(
        body,
        mesh=mesh,
        in_specs=(P(None, None, "rad", "azi"), P("rad", "azi"), P(), P()),
        out_specs=P(None, None, "rad", "azi"),
        check_vma=False,
    )
```

```python
import functools

import jax
import jax.numpy as jnp
from jax import lax
from jax.experimental import pallas as pl
from jax.experimental.pallas import tpu as pltpu
from jax.sharding import PartitionSpec as P

BLOCK = 64
time_step = 0.3
MESH = pl.DeviceIdType.MESH
DEPTH = 3


def bounds_of(radii):
    return [0, radii // 4, radii * 5 // 8, radii * 7 // 8, radii]


def neighbour_rates(centre, north, south, viscosity, spin):
    width = centre.shape[-1]
    level = lax.broadcasted_iota(jnp.int32, centre.shape, 1)
    ahead = pltpu.roll(centre, width - 1, axis=2)
    behind = pltpu.roll(centre, 1, axis=2)
    above = jnp.where(level == 7, centre, pltpu.roll(centre, 7, axis=1))
    below = jnp.where(level == 0, centre, pltpu.roll(centre, 1, axis=1))
    spread = viscosity * (north + south + ahead + behind + above + below - 6.0 * centre)
    radial_grad = 0.5 * (north - south)
    azimuth_grad = 0.5 * (ahead - behind)
    rate_density = spread[0] - radial_grad[1] - azimuth_grad[2]
    rate_radial = spread[1] - radial_grad[0] + 2.0 * spin * centre[2]
    rate_azimuth = spread[2] - azimuth_grad[0] - 0.5 * spin * centre[1]
    return jnp.stack([rate_density, rate_radial, rate_azimuth])


def kernel(
    bands, sectors, chunks,
    fields_in, viscosity_in, rotation_in, shifts_in, out,
    fields, viscosity, rotation, shifts, fetched, own, side, first, second, raws, gots, staged, pack, from_ahead, from_behind,
    halo_sent, halo_got, mate_sent, mate_got, end_sent, end_got, right_sent, right_got, left_sent, left_got,
):
    radii = viscosity.shape[0]
    places = sectors // 2
    band = lax.axis_index("rad")
    sector = lax.axis_index("azi")
    place, parity = sector // 2, sector % 2
    has_up, has_down = band < bands - 1, band > 0

    def at(dr, da):
        return (lax.rem(band + dr + bands, bands), lax.rem(sector + da + sectors, sectors))

    barrier = pltpu.get_barrier_semaphore()
    greeted = [(dr, da) for dr in (-1, 0, 1) for da in (-1, 0, 1) if (dr, da) != (0, 0)]
    greeted += [(0, 2 * d - sectors) for d in range(1, places)] + [(0, -3), (0, 3)]
    for dr, da in greeted:
        pl.semaphore_signal(barrier, inc=1, device_id=at(dr, da), device_id_type=MESH)

    fetches = [
        pltpu.make_async_copy(src, dst, fetched.at[i])
        for i, (src, dst) in enumerate(
            [(fields_in, fields), (viscosity_in, viscosity), (rotation_in, rotation), (shifts_in, shifts)]
        )
    ]
    for fetch in fetches:
        fetch.start()
    for fetch in fetches:
        fetch.wait()

    lane = lax.broadcasted_iota(jnp.int32, (8, 128), 1)
    slot = ((lane + 4) // 8) % 16
    for group in range(2):
        packed = None
        for r in range(4 * group, 4 * group + 4):
            for f in range(4):
                if f < 3:
                    tile = fields[f, pl.ds(r, 8, stride=8), :]
                else:
                    tile = jnp.broadcast_to(viscosity[pl.ds(r, 1), :], (8, 128))
                own[DEPTH + r, f] = tile
                index = (r % 4) * 4 + f
                if index == 0:
                    packed = tile
                else:
                    packed = jnp.where(slot == index, pltpu.roll(tile, 8 * index, axis=1), packed)
        pack[group] = packed

    pl.semaphore_wait(barrier, len(greeted))

    def remote(src, dst, sent, got, device):
        return pltpu.make_async_remote_copy(
            src_ref=src, dst_ref=dst, send_sem=sent, recv_sem=got, device_id=device, device_id_type=MESH
        )

    def halo(index, src, dst, device):
        return remote(src, dst, halo_sent.at[index], halo_got.at[index], device)

    last = DEPTH + radii
    up = [
        halo(0, own.at[radii:last], own.at[0:DEPTH], at(1, 0)),
        halo(4, pack.at[1], from_behind.at[0, 1], at(1, 1)),
        halo(5, pack.at[1], from_ahead.at[0, 1], at(1, -1)),
    ]
    down = [
        halo(1, own.at[DEPTH:2 * DEPTH], own.at[last:last + DEPTH], at(-1, 0)),
        halo(6, pack.at[0], from_behind.at[2, 0], at(-1, 1)),
        halo(7, pack.at[0], from_ahead.at[2, 0], at(-1, -1)),
    ]
    across = [
        halo(2, pack, from_behind.at[1], at(0, 1)),
        halo(3, pack, from_ahead.at[1], at(0, -1)),
    ]
    for copy in across:
        copy.start()

    @pl.when(has_up)
    def _():
        for copy in up:
            copy.start()

    @pl.when(has_down)
    def _():
        for copy in down:
            copy.start()

    low = (lane % 8) < 4

    def unpack(dr, group, rows, shift):
        joined = jnp.where(low, from_ahead[dr, group], from_behind[dr, group])
        for r in rows:
            for f in range(4):
                index = (r % 4) * 4 + f
                side[shift + r, f] = joined if index == 0 else pltpu.roll(joined, 128 - 8 * index, axis=1)

    for copy in across:
        copy.wait_recv()
    unpack(1, 0, range(0, 4), DEPTH)
    unpack(1, 1, range(4, 8), DEPTH)

    @pl.when(has_down)
    def _():
        for copy in up:
            copy.wait_recv()
        unpack(0, 1, range(radii - DEPTH, radii), DEPTH - radii)

    @pl.when(jnp.logical_not(has_down))
    def _():
        own[0:DEPTH] = jnp.zeros((DEPTH, 4, 8, 128), jnp.float32)
        side[0:DEPTH] = jnp.zeros((DEPTH, 4, 8, 128), jnp.float32)

    @pl.when(has_up)
    def _():
        for copy in down:
            copy.wait_recv()
        unpack(2, 0, range(0, DEPTH), last)

    @pl.when(jnp.logical_not(has_up))
    def _():
        own[last:last + DEPTH] = jnp.zeros((DEPTH, 4, 8, 128), jnp.float32)
        side[last:last + DEPTH] = jnp.zeros((DEPTH, 4, 8, 128), jnp.float32)

    def start_row(i):
        return jnp.concatenate([own[i, 0:3], side[i, 0:3]], axis=2)

    def row_facts(i):
        row = band * radii + i - DEPTH
        inside = jnp.logical_and(row >= 0, row < bands * radii)
        spin = rotation[jnp.clip(row, 0, bands * radii - 1)]
        return inside, spin, jnp.concatenate([own[i, 3], side[i, 3]], axis=1)

    def first_row(i, _):
        inside, spin, thick = row_facts(i)
        centre = start_row(i)
        rate = neighbour_rates(centre, start_row(i + 1), start_row(i - 1), thick, spin)
        first[i] = jnp.where(inside, centre + time_step * rate, 0.0)
        return 0

    lax.fori_loop(1, radii + 2 * DEPTH - 1, first_row, 0, unroll=True)

    def second_row(i, _):
        inside, spin, thick = row_facts(i)
        centre = first[i]
        rate = neighbour_rates(centre, first[i + 1], first[i - 1], thick, spin)
        second[i] = jnp.where(inside, 0.75 * start_row(i) + 0.25 * (centre + time_step * rate), 0.0)
        return 0

    lax.fori_loop(2, radii + 2 * DEPTH - 2, second_row, 0, unroll=True)

    starts = bounds_of(radii)

    def final_row(c, r):
        i = r + DEPTH
        inside, spin, thick = row_facts(i)
        centre = second[i]
        rate = neighbour_rates(centre, second[i + 1], second[i - 1], thick, spin)
        raws[c][place, r - starts[c]] = own[i, 0:3] / 3.0 + 2.0 / 3.0 * (centre + time_step * rate)[..., :128]

    def line_copy(to_right, d, c):
        held = raws[c].at[place]
        if to_right:
            return remote(held, held, right_sent.at[d, c], right_got.at[d, c], at(0, 2 * d))
        return remote(held, held, left_sent.at[d, c], left_got.at[d, c], at(0, -2 * d))

    def sends(to_right, d):
        return place + d <= places - 2 if to_right else place - d >= 1

    def gets(to_right, d):
        inner = jnp.logical_and(place >= 1, place <= places - 2)
        return jnp.logical_and(inner, place - d >= 0 if to_right else place + d <= places - 1)

    def send(c):
        for d in range(places - 2, 0, -1):
            for to_right in (True, False):
                @pl.when(sends(to_right, d))
                def _():
                    line_copy(to_right, d, c).start()

    def get(c):
        for d in range(1, places - 1):
            for to_right in (True, False):
                @pl.when(gets(to_right, d))
                def _():
                    line_copy(to_right, d, c).wait_recv()

    for c in range(chunks):
        for r in range(starts[c], starts[c + 1]):
            final_row(c, r)
        send(c)

    half = lax.broadcasted_iota(jnp.int32, (3, 8, 128), 2) < BLOCK
    total = 2 * sectors

    def sources(r, target):
        shift = shifts[0, band * radii + r]
        to_first = (2 * target - shift + total) % total // 2
        to_second = (2 * target + 1 - shift + total) % total // 2
        odd = shift % 2 == 1
        return jnp.where(odd, to_second, to_first), jnp.where(odd, to_first, to_second), odd

    def picked(c, r, target):
        low_from, high_from, _ = sources(r, target)
        return jnp.where(half, raws[c][low_from // 2, r - starts[c]], raws[c][high_from // 2, r - starts[c]])

    inner = jnp.logical_and(place >= 1, place <= places - 2)
    outer = jnp.logical_not(inner)
    beside = jnp.logical_or(place == 1, place == places - 2)
    mate = sector + 1 - 2 * parity
    end = sector + jnp.where(place == 1, -2, 2)
    end_mate = end + 1 - 2 * parity

    def mate_copy(c):
        return remote(staged[c].at[0], gots[c].at[parity], mate_sent.at[c], mate_got.at[c], (band, mate))

    def end_copy(other, c):
        target = lax.rem((end_mate if other else end) + sectors, sectors)
        return remote(
            staged[c].at[1 + other], gots[c].at[parity], end_sent.at[other, c], end_got.at[parity, c], (band, target)
        )

    def from_helper(q, c):
        return remote(gots[c].at[q], gots[c].at[q], end_sent.at[q, c], end_got.at[q, c], (band, mate))

    for c in range(chunks):
        get(c)
        rows = range(starts[c], starts[c + 1])

        @pl.when(beside)
        def _():
            for other, target in ((0, end), (1, end_mate)):
                for r in rows:
                    staged[c][1 + other, r - starts[c]] = picked(c, r, target)
                end_copy(other, c).start()

        @pl.when(inner)
        def _():
            for r in rows:
                staged[c][0, r - starts[c]] = picked(c, r, mate)
            mate_copy(c).start()
            for r in rows:
                gots[c][parity, r - starts[c]] = picked(c, r, sector)

    for c in range(chunks):
        @pl.when(inner)
        def _():
            mate_copy(c).wait_recv()

        @pl.when(outer)
        def _():
            for q in range(2):
                from_helper(q, c).wait_recv()

        for r in range(starts[c], starts[c + 1]):
            low_from, high_from, odd = sources(r, sector)
            moved = jnp.where(half, gots[c][low_from % 2, r - starts[c]], gots[c][high_from % 2, r - starts[c]])
            moved = jnp.where(odd, pltpu.roll(moved, BLOCK, axis=2), moved)
            for f in range(3):
                out[f, pl.ds(r, 8, stride=8), :] = moved[f]

    for copy in across:
        copy.wait_send()

    @pl.when(has_up)
    def _():
        for copy in up:
            copy.wait_send()

    @pl.when(has_down)
    def _():
        for copy in down:
            copy.wait_send()

    for c in range(chunks):
        @pl.when(beside)
        def _():
            for other in range(2):
                end_copy(other, c).wait_send()

        @pl.when(inner)
        def _():
            mate_copy(c).wait_send()

    for d in range(1, places - 1):
        for c in range(chunks):
            for to_right in (True, False):
                @pl.when(sends(to_right, d))
                def _():
                    line_copy(to_right, d, c).wait_send()


def body(fields, viscosity, rotation, shift_blocks):
    bands, sectors = lax.axis_size("rad"), lax.axis_size("azi")
    kinds, height, radii, width = fields.shape
    places = sectors // 2
    starts = bounds_of(radii)
    chunks = len(starts) - 1
    sizes = [starts[c + 1] - starts[c] for c in range(chunks)]
    rows = radii + 2 * DEPTH
    steps = places - 1
    vmem = lambda *shape: pltpu.VMEM(shape, jnp.float32)
    dma = lambda *shape: pltpu.SemaphoreType.DMA(shape)
    moved = pl.pallas_call(
        functools.partial(kernel, bands, sectors, chunks),
        out_shape=pltpu.VMEM((kinds, height * radii, width), jnp.float32),
        in_specs=[pl.BlockSpec(memory_space=pltpu.HBM)] * 4,
        out_specs=pl.BlockSpec(memory_space=pltpu.VMEM),
        scratch_shapes=[
            vmem(kinds, height * radii, width), vmem(radii, width),
            pltpu.SMEM(rotation.shape, jnp.float32), pltpu.SMEM(shift_blocks.shape, jnp.int32), dma(4),
            vmem(rows, 4, 8, 128), vmem(rows, 4, 8, 128),
            vmem(rows, 3, 8, 256), vmem(rows, 3, 8, 256),
            [vmem(places, size, 3, 8, 128) for size in sizes],
            [vmem(2, size, 3, 8, 128) for size in sizes],
            [vmem(3, size, 3, 8, 128) for size in sizes],
            vmem(2, 8, 128), vmem(3, 2, 8, 128), vmem(3, 2, 8, 128),
            dma(8), dma(8), dma(chunks), dma(chunks), dma(2, chunks), dma(2, chunks),
            dma(steps, chunks), dma(steps, chunks), dma(steps, chunks), dma(steps, chunks),
        ],
        compiler_params=pltpu.CompilerParams(collective_id=0, has_side_effects=True, vmem_limit_bytes=56 * 2**20),
        name="disc_step",
    )(fields.reshape(kinds, height * radii, width), viscosity, rotation, shift_blocks)
    return moved.reshape(fields.shape)


def solution(mesh):
    return jax.shard_map(
        body,
        mesh=mesh,
        in_specs=(P(None, None, "rad", "azi"), P("rad", "azi"), P(), P()),
        out_specs=P(None, None, "rad", "azi"),
        check_vma=False,
    )
```

```python
import functools

import jax
import jax.numpy as jnp
from jax import lax
from jax.experimental import pallas as pl
from jax.experimental.pallas import tpu as pltpu
from jax.sharding import PartitionSpec as P

BLOCK = 64
time_step = 0.3
MESH = pl.DeviceIdType.MESH
DEPTH = 3


def bounds_of(radii):
    return [0, radii // 2, radii]


def neighbour_rates(centre, north, south, viscosity, spin):
    width = centre.shape[-1]
    level = lax.broadcasted_iota(jnp.int32, centre.shape, 1)
    ahead = pltpu.roll(centre, width - 1, axis=2)
    behind = pltpu.roll(centre, 1, axis=2)
    above = jnp.where(level == 7, centre, pltpu.roll(centre, 7, axis=1))
    below = jnp.where(level == 0, centre, pltpu.roll(centre, 1, axis=1))
    spread = viscosity * (north + south + ahead + behind + above + below - 6.0 * centre)
    radial_grad = 0.5 * (north - south)
    azimuth_grad = 0.5 * (ahead - behind)
    rate_density = spread[0] - radial_grad[1] - azimuth_grad[2]
    rate_radial = spread[1] - radial_grad[0] + 2.0 * spin * centre[2]
    rate_azimuth = spread[2] - azimuth_grad[0] - 0.5 * spin * centre[1]
    return jnp.stack([rate_density, rate_radial, rate_azimuth])


def kernel(
    bands, sectors, chunks,
    fields_in, viscosity_in, rotation_in, shifts_in, out,
    fields, viscosity, rotation, shifts, fetched, own, side, first, second, raws, gots, staged, pack, from_ahead, from_behind,
    halo_sent, halo_got, mate_sent, mate_got, end_sent, end_got, right_sent, right_got, left_sent, left_got,
):
    radii = viscosity.shape[0]
    places = sectors // 2
    band = lax.axis_index("rad")
    sector = lax.axis_index("azi")
    place, parity = sector // 2, sector % 2
    has_up, has_down = band < bands - 1, band > 0

    def at(dr, da):
        return (lax.rem(band + dr + bands, bands), lax.rem(sector + da + sectors, sectors))

    barrier = pltpu.get_barrier_semaphore()
    greeted = [(dr, da) for dr in (-1, 0, 1) for da in (-1, 0, 1) if (dr, da) != (0, 0)]
    greeted += [(0, 2 * d - sectors) for d in range(1, places)] + [(0, -3), (0, 3)]
    for dr, da in greeted:
        pl.semaphore_signal(barrier, inc=1, device_id=at(dr, da), device_id_type=MESH)

    fetches = [
        pltpu.make_async_copy(src, dst, fetched.at[i])
        for i, (src, dst) in enumerate(
            [(fields_in, fields), (viscosity_in, viscosity), (rotation_in, rotation), (shifts_in, shifts)]
        )
    ]
    for fetch in fetches:
        fetch.start()
    for fetch in fetches:
        fetch.wait()

    lane = lax.broadcasted_iota(jnp.int32, (8, 128), 1)
    slot = ((lane + 4) // 8) % 16
    for group in range(2):
        packed = None
        for r in range(4 * group, 4 * group + 4):
            for f in range(4):
                if f < 3:
                    tile = fields[f, pl.ds(r, 8, stride=8), :]
                else:
                    tile = jnp.broadcast_to(viscosity[pl.ds(r, 1), :], (8, 128))
                own[DEPTH + r, f] = tile
                index = (r % 4) * 4 + f
                if index == 0:
                    packed = tile
                else:
                    packed = jnp.where(slot == index, pltpu.roll(tile, 8 * index, axis=1), packed)
        pack[group] = packed

    pl.semaphore_wait(barrier, len(greeted))

    def remote(src, dst, sent, got, device):
        return pltpu.make_async_remote_copy(
            src_ref=src, dst_ref=dst, send_sem=sent, recv_sem=got, device_id=device, device_id_type=MESH
        )

    def halo(index, src, dst, device):
        return remote(src, dst, halo_sent.at[index], halo_got.at[index], device)

    last = DEPTH + radii
    up = [
        halo(0, own.at[radii:last], own.at[0:DEPTH], at(1, 0)),
        halo(4, pack.at[1], from_behind.at[0, 1], at(1, 1)),
        halo(5, pack.at[1], from_ahead.at[0, 1], at(1, -1)),
    ]
    down = [
        halo(1, own.at[DEPTH:2 * DEPTH], own.at[last:last + DEPTH], at(-1, 0)),
        halo(6, pack.at[0], from_behind.at[2, 0], at(-1, 1)),
        halo(7, pack.at[0], from_ahead.at[2, 0], at(-1, -1)),
    ]
    across = [
        halo(2, pack, from_behind.at[1], at(0, 1)),
        halo(3, pack, from_ahead.at[1], at(0, -1)),
    ]
    for copy in across:
        copy.start()

    @pl.when(has_up)
    def _():
        for copy in up:
            copy.start()

    @pl.when(has_down)
    def _():
        for copy in down:
            copy.start()

    low = (lane % 8) < 4

    def unpack(dr, group, rows, shift):
        joined = jnp.where(low, from_ahead[dr, group], from_behind[dr, group])
        for r in rows:
            for f in range(4):
                index = (r % 4) * 4 + f
                side[shift + r, f] = joined if index == 0 else pltpu.roll(joined, 128 - 8 * index, axis=1)

    for copy in across:
        copy.wait_recv()
    unpack(1, 0, range(0, 4), DEPTH)
    unpack(1, 1, range(4, 8), DEPTH)

    @pl.when(has_down)
    def _():
        for copy in up:
            copy.wait_recv()
        unpack(0, 1, range(radii - DEPTH, radii), DEPTH - radii)

    @pl.when(jnp.logical_not(has_down))
    def _():
        own[0:DEPTH] = jnp.zeros((DEPTH, 4, 8, 128), jnp.float32)
        side[0:DEPTH] = jnp.zeros((DEPTH, 4, 8, 128), jnp.float32)

    @pl.when(has_up)
    def _():
        for copy in down:
            copy.wait_recv()
        unpack(2, 0, range(0, DEPTH), last)

    @pl.when(jnp.logical_not(has_up))
    def _():
        own[last:last + DEPTH] = jnp.zeros((DEPTH, 4, 8, 128), jnp.float32)
        side[last:last + DEPTH] = jnp.zeros((DEPTH, 4, 8, 128), jnp.float32)

    def start_row(i):
        return jnp.concatenate([own[i, 0:3], side[i, 0:3]], axis=2)

    def row_facts(i):
        row = band * radii + i - DEPTH
        inside = jnp.logical_and(row >= 0, row < bands * radii)
        spin = rotation[jnp.clip(row, 0, bands * radii - 1)]
        return inside, spin, jnp.concatenate([own[i, 3], side[i, 3]], axis=1)

    def first_row(i, _):
        inside, spin, thick = row_facts(i)
        centre = start_row(i)
        rate = neighbour_rates(centre, start_row(i + 1), start_row(i - 1), thick, spin)
        first[i] = jnp.where(inside, centre + time_step * rate, 0.0)
        return 0

    lax.fori_loop(1, radii + 2 * DEPTH - 1, first_row, 0, unroll=True)

    def second_row(i, _):
        inside, spin, thick = row_facts(i)
        centre = first[i]
        rate = neighbour_rates(centre, first[i + 1], first[i - 1], thick, spin)
        second[i] = jnp.where(inside, 0.75 * start_row(i) + 0.25 * (centre + time_step * rate), 0.0)
        return 0

    lax.fori_loop(2, radii + 2 * DEPTH - 2, second_row, 0, unroll=True)

    starts = bounds_of(radii)

    def final_row(c, r):
        i = r + DEPTH
        inside, spin, thick = row_facts(i)
        centre = second[i]
        rate = neighbour_rates(centre, second[i + 1], second[i - 1], thick, spin)
        raws[c][place, r - starts[c]] = own[i, 0:3] / 3.0 + 2.0 / 3.0 * (centre + time_step * rate)[..., :128]

    def line_copy(to_right, d, c):
        held = raws[c].at[place]
        if to_right:
            return remote(held, held, right_sent.at[d, c], right_got.at[d, c], at(0, 2 * d))
        return remote(held, held, left_sent.at[d, c], left_got.at[d, c], at(0, -2 * d))

    def sends(to_right, d):
        return place + d <= places - 2 if to_right else place - d >= 1

    def gets(to_right, d):
        inner = jnp.logical_and(place >= 1, place <= places - 2)
        return jnp.logical_and(inner, place - d >= 0 if to_right else place + d <= places - 1)

    def send(c):
        for d in range(places - 2, 0, -1):
            for to_right in (True, False):
                @pl.when(sends(to_right, d))
                def _():
                    line_copy(to_right, d, c).start()

    def get(c):
        for d in range(1, places - 1):
            for to_right in (True, False):
                @pl.when(gets(to_right, d))
                def _():
                    line_copy(to_right, d, c).wait_recv()

    for c in range(chunks):
        for r in range(starts[c], starts[c + 1]):
            final_row(c, r)
        send(c)

    half = lax.broadcasted_iota(jnp.int32, (3, 8, 128), 2) < BLOCK
    total = 2 * sectors

    def sources(r, target):
        shift = shifts[0, band * radii + r]
        to_first = (2 * target - shift + total) % total // 2
        to_second = (2 * target + 1 - shift + total) % total // 2
        odd = shift % 2 == 1
        return jnp.where(odd, to_second, to_first), jnp.where(odd, to_first, to_second), odd

    def picked(c, r, target):
        low_from, high_from, _ = sources(r, target)
        return jnp.where(half, raws[c][low_from // 2, r - starts[c]], raws[c][high_from // 2, r - starts[c]])

    inner = jnp.logical_and(place >= 1, place <= places - 2)
    outer = jnp.logical_not(inner)
    beside = jnp.logical_or(place == 1, place == places - 2)
    mate = sector + 1 - 2 * parity
    end = sector + jnp.where(place == 1, -2, 2)
    end_mate = end + 1 - 2 * parity

    def mate_copy(c):
        return remote(staged[c].at[0], gots[c].at[parity], mate_sent.at[c], mate_got.at[c], (band, mate))

    def end_copy(other, c):
        target = lax.rem((end_mate if other else end) + sectors, sectors)
        return remote(
            staged[c].at[1 + other], gots[c].at[parity], end_sent.at[other, c], end_got.at[parity, c], (band, target)
        )

    def from_helper(q, c):
        return remote(gots[c].at[q], gots[c].at[q], end_sent.at[q, c], end_got.at[q, c], (band, mate))

    for c in range(chunks):
        get(c)
        rows = range(starts[c], starts[c + 1])

        @pl.when(beside)
        def _():
            for other, target in ((0, end), (1, end_mate)):
                for r in rows:
                    staged[c][1 + other, r - starts[c]] = picked(c, r, target)
                end_copy(other, c).start()

        @pl.when(inner)
        def _():
            for r in rows:
                staged[c][0, r - starts[c]] = picked(c, r, mate)
            mate_copy(c).start()
            for r in rows:
                gots[c][parity, r - starts[c]] = picked(c, r, sector)

    for c in range(chunks):
        @pl.when(inner)
        def _():
            mate_copy(c).wait_recv()

        @pl.when(outer)
        def _():
            for q in range(2):
                from_helper(q, c).wait_recv()

        for r in range(starts[c], starts[c + 1]):
            low_from, high_from, odd = sources(r, sector)
            moved = jnp.where(half, gots[c][low_from % 2, r - starts[c]], gots[c][high_from % 2, r - starts[c]])
            moved = jnp.where(odd, pltpu.roll(moved, BLOCK, axis=2), moved)
            for f in range(3):
                out[f, pl.ds(r, 8, stride=8), :] = moved[f]

    for copy in across:
        copy.wait_send()

    @pl.when(has_up)
    def _():
        for copy in up:
            copy.wait_send()

    @pl.when(has_down)
    def _():
        for copy in down:
            copy.wait_send()

    for c in range(chunks):
        @pl.when(beside)
        def _():
            for other in range(2):
                end_copy(other, c).wait_send()

        @pl.when(inner)
        def _():
            mate_copy(c).wait_send()

    for d in range(1, places - 1):
        for c in range(chunks):
            for to_right in (True, False):
                @pl.when(sends(to_right, d))
                def _():
                    line_copy(to_right, d, c).wait_send()


def body(fields, viscosity, rotation, shift_blocks):
    bands, sectors = lax.axis_size("rad"), lax.axis_size("azi")
    kinds, height, radii, width = fields.shape
    places = sectors // 2
    starts = bounds_of(radii)
    chunks = len(starts) - 1
    sizes = [starts[c + 1] - starts[c] for c in range(chunks)]
    rows = radii + 2 * DEPTH
    steps = places - 1
    vmem = lambda *shape: pltpu.VMEM(shape, jnp.float32)
    dma = lambda *shape: pltpu.SemaphoreType.DMA(shape)
    moved = pl.pallas_call(
        functools.partial(kernel, bands, sectors, chunks),
        out_shape=pltpu.VMEM((kinds, height * radii, width), jnp.float32),
        in_specs=[pl.BlockSpec(memory_space=pltpu.HBM)] * 4,
        out_specs=pl.BlockSpec(memory_space=pltpu.VMEM),
        scratch_shapes=[
            vmem(kinds, height * radii, width), vmem(radii, width),
            pltpu.SMEM(rotation.shape, jnp.float32), pltpu.SMEM(shift_blocks.shape, jnp.int32), dma(4),
            vmem(rows, 4, 8, 128), vmem(rows, 4, 8, 128),
            vmem(rows, 3, 8, 256), vmem(rows, 3, 8, 256),
            [vmem(places, size, 3, 8, 128) for size in sizes],
            [vmem(2, size, 3, 8, 128) for size in sizes],
            [vmem(3, size, 3, 8, 128) for size in sizes],
            vmem(2, 8, 128), vmem(3, 2, 8, 128), vmem(3, 2, 8, 128),
            dma(8), dma(8), dma(chunks), dma(chunks), dma(2, chunks), dma(2, chunks),
            dma(steps, chunks), dma(steps, chunks), dma(steps, chunks), dma(steps, chunks),
        ],
        compiler_params=pltpu.CompilerParams(collective_id=0, has_side_effects=True, vmem_limit_bytes=56 * 2**20),
        name="disc_step",
    )(fields.reshape(kinds, height * radii, width), viscosity, rotation, shift_blocks)
    return moved.reshape(fields.shape)


def solution(mesh):
    return jax.shard_map(
        body,
        mesh=mesh,
        in_specs=(P(None, None, "rad", "azi"), P("rad", "azi"), P(), P()),
        out_specs=P(None, None, "rad", "azi"),
        check_vma=False,
    )
```

```python
import functools

import jax
import jax.numpy as jnp
from jax import lax
from jax.experimental import pallas as pl
from jax.experimental.pallas import tpu as pltpu
from jax.sharding import PartitionSpec as P

BLOCK = 64
time_step = 0.3
MESH = pl.DeviceIdType.MESH
DEPTH = 3


def bounds_of(radii):
    return [radii * c // 4 for c in range(5)]


def neighbour_rates(centre, north, south, viscosity, spin):
    width = centre.shape[-1]
    level = lax.broadcasted_iota(jnp.int32, centre.shape, 1)
    ahead = pltpu.roll(centre, width - 1, axis=2)
    behind = pltpu.roll(centre, 1, axis=2)
    above = jnp.where(level == 7, centre, pltpu.roll(centre, 7, axis=1))
    below = jnp.where(level == 0, centre, pltpu.roll(centre, 1, axis=1))
    spread = viscosity * (north + south + ahead + behind + above + below - 6.0 * centre)
    radial_grad = 0.5 * (north - south)
    azimuth_grad = 0.5 * (ahead - behind)
    rate_density = spread[0] - radial_grad[1] - azimuth_grad[2]
    rate_radial = spread[1] - radial_grad[0] + 2.0 * spin * centre[2]
    rate_azimuth = spread[2] - azimuth_grad[0] - 0.5 * spin * centre[1]
    return jnp.stack([rate_density, rate_radial, rate_azimuth])


def kernel(
    bands, sectors, chunks,
    fields_in, viscosity_in, rotation_in, shifts_in, out,
    fields, viscosity, rotation, shifts, fetched, own, side, first, second, raws, gots, staged, pack, from_ahead, from_behind,
    halo_sent, halo_got, mate_sent, mate_got, end_sent, end_got, right_sent, right_got, left_sent, left_got,
):
    radii = viscosity.shape[0]
    places = sectors // 2
    band = lax.axis_index("rad")
    sector = lax.axis_index("azi")
    place, parity = sector // 2, sector % 2
    has_up, has_down = band < bands - 1, band > 0

    def at(dr, da):
        return (lax.rem(band + dr + bands, bands), lax.rem(sector + da + sectors, sectors))

    barrier = pltpu.get_barrier_semaphore()
    greeted = [(dr, da) for dr in (-1, 0, 1) for da in (-1, 0, 1) if (dr, da) != (0, 0)]
    greeted += [(0, 2 * d - sectors) for d in range(1, places)] + [(0, -3), (0, 3)]
    for dr, da in greeted:
        pl.semaphore_signal(barrier, inc=1, device_id=at(dr, da), device_id_type=MESH)

    fetches = [
        pltpu.make_async_copy(src, dst, fetched.at[i])
        for i, (src, dst) in enumerate(
            [(fields_in, fields), (viscosity_in, viscosity), (rotation_in, rotation), (shifts_in, shifts)]
        )
    ]
    for fetch in fetches:
        fetch.start()
    for fetch in fetches:
        fetch.wait()

    lane = lax.broadcasted_iota(jnp.int32, (8, 128), 1)
    slot = ((lane + 4) // 8) % 16
    for group in range(2):
        packed = None
        for r in range(4 * group, 4 * group + 4):
            for f in range(4):
                if f < 3:
                    tile = fields[f, pl.ds(r, 8, stride=8), :]
                else:
                    tile = jnp.broadcast_to(viscosity[pl.ds(r, 1), :], (8, 128))
                own[DEPTH + r, f] = tile
                index = (r % 4) * 4 + f
                if index == 0:
                    packed = tile
                else:
                    packed = jnp.where(slot == index, pltpu.roll(tile, 8 * index, axis=1), packed)
        pack[group] = packed

    pl.semaphore_wait(barrier, len(greeted))

    def remote(src, dst, sent, got, device):
        return pltpu.make_async_remote_copy(
            src_ref=src, dst_ref=dst, send_sem=sent, recv_sem=got, device_id=device, device_id_type=MESH
        )

    def halo(index, src, dst, device):
        return remote(src, dst, halo_sent.at[index], halo_got.at[index], device)

    last = DEPTH + radii
    up = [
        halo(0, own.at[radii:last], own.at[0:DEPTH], at(1, 0)),
        halo(4, pack.at[1], from_behind.at[0, 1], at(1, 1)),
        halo(5, pack.at[1], from_ahead.at[0, 1], at(1, -1)),
    ]
    down = [
        halo(1, own.at[DEPTH:2 * DEPTH], own.at[last:last + DEPTH], at(-1, 0)),
        halo(6, pack.at[0], from_behind.at[2, 0], at(-1, 1)),
        halo(7, pack.at[0], from_ahead.at[2, 0], at(-1, -1)),
    ]
    across = [
        halo(2, pack, from_behind.at[1], at(0, 1)),
        halo(3, pack, from_ahead.at[1], at(0, -1)),
    ]
    for copy in across:
        copy.start()

    @pl.when(has_up)
    def _():
        for copy in up:
            copy.start()

    @pl.when(has_down)
    def _():
        for copy in down:
            copy.start()

    low = (lane % 8) < 4

    def unpack(dr, group, rows, shift):
        joined = jnp.where(low, from_ahead[dr, group], from_behind[dr, group])
        for r in rows:
            for f in range(4):
                index = (r % 4) * 4 + f
                side[shift + r, f] = joined if index == 0 else pltpu.roll(joined, 128 - 8 * index, axis=1)

    for copy in across:
        copy.wait_recv()
    unpack(1, 0, range(0, 4), DEPTH)
    unpack(1, 1, range(4, 8), DEPTH)

    @pl.when(has_down)
    def _():
        for copy in up:
            copy.wait_recv()
        unpack(0, 1, range(radii - DEPTH, radii), DEPTH - radii)

    @pl.when(jnp.logical_not(has_down))
    def _():
        own[0:DEPTH] = jnp.zeros((DEPTH, 4, 8, 128), jnp.float32)
        side[0:DEPTH] = jnp.zeros((DEPTH, 4, 8, 128), jnp.float32)

    def take_upper_halo():
        @pl.when(has_up)
        def _():
            for copy in down:
                copy.wait_recv()
            unpack(2, 0, range(0, DEPTH), last)

        @pl.when(jnp.logical_not(has_up))
        def _():
            own[last:last + DEPTH] = jnp.zeros((DEPTH, 4, 8, 128), jnp.float32)
            side[last:last + DEPTH] = jnp.zeros((DEPTH, 4, 8, 128), jnp.float32)

    def start_row(i):
        return jnp.concatenate([own[i, 0:3], side[i, 0:3]], axis=2)

    def row_facts(i):
        row = band * radii + i - DEPTH
        inside = jnp.logical_and(row >= 0, row < bands * radii)
        spin = rotation[jnp.clip(row, 0, bands * radii - 1)]
        return inside, spin, jnp.concatenate([own[i, 3], side[i, 3]], axis=1)

    def first_row(i, _):
        inside, spin, thick = row_facts(i)
        centre = start_row(i)
        rate = neighbour_rates(centre, start_row(i + 1), start_row(i - 1), thick, spin)
        first[i] = jnp.where(inside, centre + time_step * rate, 0.0)
        return 0

    def second_row(i, _):
        inside, spin, thick = row_facts(i)
        centre = first[i]
        rate = neighbour_rates(centre, first[i + 1], first[i - 1], thick, spin)
        second[i] = jnp.where(inside, 0.75 * start_row(i) + 0.25 * (centre + time_step * rate), 0.0)
        return 0

    starts = bounds_of(radii)

    def final_row(c, r):
        i = r + DEPTH
        inside, spin, thick = row_facts(i)
        centre = second[i]
        rate = neighbour_rates(centre, second[i + 1], second[i - 1], thick, spin)
        raws[c][place, r - starts[c]] = own[i, 0:3] / 3.0 + 2.0 / 3.0 * (centre + time_step * rate)[..., :128]

    def line_copy(to_right, d, c):
        held = raws[c].at[place]
        if to_right:
            return remote(held, held, right_sent.at[d, c], right_got.at[d, c], at(0, 2 * d))
        return remote(held, held, left_sent.at[d, c], left_got.at[d, c], at(0, -2 * d))

    def sends(to_right, d):
        return place + d <= places - 2 if to_right else place - d >= 1

    def gets(to_right, d):
        inner = jnp.logical_and(place >= 1, place <= places - 2)
        return jnp.logical_and(inner, place - d >= 0 if to_right else place + d <= places - 1)

    def send(c):
        for d in range(places - 2, 0, -1):
            for to_right in (True, False):
                @pl.when(sends(to_right, d))
                def _():
                    line_copy(to_right, d, c).start()

    def get(c):
        for d in range(1, places - 1):
            for to_right in (True, False):
                @pl.when(gets(to_right, d))
                def _():
                    line_copy(to_right, d, c).wait_recv()

    first_end, second_end = 1, 2
    for c in range(chunks):
        need_first = min(starts[c + 1] + DEPTH + 2, last + DEPTH - 1)
        need_second = min(starts[c + 1] + DEPTH + 1, last + DEPTH - 2)
        if first_end < last <= need_first:
            take_upper_halo()
        lax.fori_loop(first_end, need_first, first_row, 0, unroll=True)
        lax.fori_loop(second_end, need_second, second_row, 0, unroll=True)
        first_end, second_end = need_first, need_second
        for r in range(starts[c], starts[c + 1]):
            final_row(c, r)
        send(c)

    half = lax.broadcasted_iota(jnp.int32, (3, 8, 128), 2) < BLOCK
    total = 2 * sectors

    def sources(r, target):
        shift = shifts[0, band * radii + r]
        to_first = (2 * target - shift + total) % total // 2
        to_second = (2 * target + 1 - shift + total) % total // 2
        odd = shift % 2 == 1
        return jnp.where(odd, to_second, to_first), jnp.where(odd, to_first, to_second), odd

    def picked(c, r, target):
        low_from, high_from, _ = sources(r, target)
        return jnp.where(half, raws[c][low_from // 2, r - starts[c]], raws[c][high_from // 2, r - starts[c]])

    inner = jnp.logical_and(place >= 1, place <= places - 2)
    outer = jnp.logical_not(inner)
    beside = jnp.logical_or(place == 1, place == places - 2)
    mate = sector + 1 - 2 * parity
    end = sector + jnp.where(place == 1, -2, 2)
    end_mate = end + 1 - 2 * parity

    def mate_copy(c):
        return remote(staged[c].at[0], gots[c].at[parity], mate_sent.at[c], mate_got.at[c], (band, mate))

    def end_copy(other, c):
        target = lax.rem((end_mate if other else end) + sectors, sectors)
        return remote(
            staged[c].at[1 + other], gots[c].at[parity], end_sent.at[other, c], end_got.at[parity, c], (band, target)
        )

    def from_helper(q, c):
        return remote(gots[c].at[q], gots[c].at[q], end_sent.at[q, c], end_got.at[q, c], (band, mate))

    for c in range(chunks):
        get(c)
        rows = range(starts[c], starts[c + 1])

        @pl.when(beside)
        def _():
            for other, target in ((0, end), (1, end_mate)):
                for r in rows:
                    staged[c][1 + other, r - starts[c]] = picked(c, r, target)
                end_copy(other, c).start()

        @pl.when(inner)
        def _():
            for r in rows:
                staged[c][0, r - starts[c]] = picked(c, r, mate)
            mate_copy(c).start()
            for r in rows:
                gots[c][parity, r - starts[c]] = picked(c, r, sector)

    for c in range(chunks):
        @pl.when(inner)
        def _():
            mate_copy(c).wait_recv()

        @pl.when(outer)
        def _():
            for q in range(2):
                from_helper(q, c).wait_recv()

        for r in range(starts[c], starts[c + 1]):
            low_from, high_from, odd = sources(r, sector)
            moved = jnp.where(half, gots[c][low_from % 2, r - starts[c]], gots[c][high_from % 2, r - starts[c]])
            moved = jnp.where(odd, pltpu.roll(moved, BLOCK, axis=2), moved)
            for f in range(3):
                out[f, pl.ds(r, 8, stride=8), :] = moved[f]

    for copy in across:
        copy.wait_send()

    @pl.when(has_up)
    def _():
        for copy in up:
            copy.wait_send()

    @pl.when(has_down)
    def _():
        for copy in down:
            copy.wait_send()

    for c in range(chunks):
        @pl.when(beside)
        def _():
            for other in range(2):
                end_copy(other, c).wait_send()

        @pl.when(inner)
        def _():
            mate_copy(c).wait_send()

    for d in range(1, places - 1):
        for c in range(chunks):
            for to_right in (True, False):
                @pl.when(sends(to_right, d))
                def _():
                    line_copy(to_right, d, c).wait_send()


def body(fields, viscosity, rotation, shift_blocks):
    bands, sectors = lax.axis_size("rad"), lax.axis_size("azi")
    kinds, height, radii, width = fields.shape
    places = sectors // 2
    starts = bounds_of(radii)
    chunks = len(starts) - 1
    sizes = [starts[c + 1] - starts[c] for c in range(chunks)]
    rows = radii + 2 * DEPTH
    steps = places - 1
    vmem = lambda *shape: pltpu.VMEM(shape, jnp.float32)
    dma = lambda *shape: pltpu.SemaphoreType.DMA(shape)
    moved = pl.pallas_call(
        functools.partial(kernel, bands, sectors, chunks),
        out_shape=pltpu.VMEM((kinds, height * radii, width), jnp.float32),
        in_specs=[pl.BlockSpec(memory_space=pltpu.HBM)] * 4,
        out_specs=pl.BlockSpec(memory_space=pltpu.VMEM),
        scratch_shapes=[
            vmem(kinds, height * radii, width), vmem(radii, width),
            pltpu.SMEM(rotation.shape, jnp.float32), pltpu.SMEM(shift_blocks.shape, jnp.int32), dma(4),
            vmem(rows, 4, 8, 128), vmem(rows, 4, 8, 128),
            vmem(rows, 3, 8, 256), vmem(rows, 3, 8, 256),
            [vmem(places, size, 3, 8, 128) for size in sizes],
            [vmem(2, size, 3, 8, 128) for size in sizes],
            [vmem(3, size, 3, 8, 128) for size in sizes],
            vmem(2, 8, 128), vmem(3, 2, 8, 128), vmem(3, 2, 8, 128),
            dma(8), dma(8), dma(chunks), dma(chunks), dma(2, chunks), dma(2, chunks),
            dma(steps, chunks), dma(steps, chunks), dma(steps, chunks), dma(steps, chunks),
        ],
        compiler_params=pltpu.CompilerParams(collective_id=0, has_side_effects=True, vmem_limit_bytes=56 * 2**20),
        name="disc_step",
    )(fields.reshape(kinds, height * radii, width), viscosity, rotation, shift_blocks)
    return moved.reshape(fields.shape)


def solution(mesh):
    return jax.shard_map(
        body,
        mesh=mesh,
        in_specs=(P(None, None, "rad", "azi"), P("rad", "azi"), P(), P()),
        out_specs=P(None, None, "rad", "azi"),
        check_vma=False,
    )
```

```python
import functools

import jax
import jax.numpy as jnp
from jax import lax
from jax.experimental import pallas as pl
from jax.experimental.pallas import tpu as pltpu
from jax.sharding import PartitionSpec as P

BLOCK = 64
time_step = 0.3
MESH = pl.DeviceIdType.MESH
DEPTH = 3


def bounds_of(radii):
    return [0, radii // 2, radii]


def neighbour_rates(centre, north, south, viscosity, spin):
    width = centre.shape[-1]
    level = lax.broadcasted_iota(jnp.int32, centre.shape, 1)
    ahead = pltpu.roll(centre, width - 1, axis=2)
    behind = pltpu.roll(centre, 1, axis=2)
    above = jnp.where(level == 7, centre, pltpu.roll(centre, 7, axis=1))
    below = jnp.where(level == 0, centre, pltpu.roll(centre, 1, axis=1))
    spread = viscosity * (north + south + ahead + behind + above + below - 6.0 * centre)
    radial_grad = 0.5 * (north - south)
    azimuth_grad = 0.5 * (ahead - behind)
    rate_density = spread[0] - radial_grad[1] - azimuth_grad[2]
    rate_radial = spread[1] - radial_grad[0] + 2.0 * spin * centre[2]
    rate_azimuth = spread[2] - azimuth_grad[0] - 0.5 * spin * centre[1]
    return jnp.stack([rate_density, rate_radial, rate_azimuth])


def kernel(
    bands, sectors, chunks,
    fields_in, viscosity_in, rotation_in, shifts_in, out,
    fields, viscosity, rotation, shifts, fetched, own, side, first, second, raws, gots, staged, pack, from_ahead, from_behind,
    halo_sent, halo_got, mate_sent, mate_got, end_sent, end_got, right_sent, right_got, left_sent, left_got,
):
    radii = viscosity.shape[0]
    places = sectors // 2
    band = lax.axis_index("rad")
    sector = lax.axis_index("azi")
    place, parity = sector // 2, sector % 2
    has_up, has_down = band < bands - 1, band > 0

    def at(dr, da):
        return (lax.rem(band + dr + bands, bands), lax.rem(sector + da + sectors, sectors))

    barrier = pltpu.get_barrier_semaphore()
    greeted = [(dr, da) for dr in (-1, 0, 1) for da in (-1, 0, 1) if (dr, da) != (0, 0)]
    greeted += [(0, 2 * d - sectors) for d in range(1, places)] + [(0, -3), (0, 3)]
    for dr, da in greeted:
        pl.semaphore_signal(barrier, inc=1, device_id=at(dr, da), device_id_type=MESH)

    fetches = [
        pltpu.make_async_copy(src, dst, fetched.at[i])
        for i, (src, dst) in enumerate(
            [(fields_in, fields), (viscosity_in, viscosity), (rotation_in, rotation), (shifts_in, shifts)]
        )
    ]
    for fetch in fetches:
        fetch.start()
    for fetch in fetches:
        fetch.wait()

    lane = lax.broadcasted_iota(jnp.int32, (8, 128), 1)
    slot = ((lane + 4) // 8) % 16
    for group in range(2):
        packed = None
        for r in range(4 * group, 4 * group + 4):
            for f in range(4):
                if f < 3:
                    tile = fields[f, pl.ds(r, 8, stride=8), :]
                else:
                    tile = jnp.broadcast_to(viscosity[pl.ds(r, 1), :], (8, 128))
                own[DEPTH + r, f] = tile
                index = (r % 4) * 4 + f
                if index == 0:
                    packed = tile
                else:
                    packed = jnp.where(slot == index, pltpu.roll(tile, 8 * index, axis=1), packed)
        pack[group] = packed

    pl.semaphore_wait(barrier, len(greeted))

    def remote(src, dst, sent, got, device):
        return pltpu.make_async_remote_copy(
            src_ref=src, dst_ref=dst, send_sem=sent, recv_sem=got, device_id=device, device_id_type=MESH
        )

    def halo(index, src, dst, device):
        return remote(src, dst, halo_sent.at[index], halo_got.at[index], device)

    last = DEPTH + radii
    up = [
        halo(0, own.at[radii:last], own.at[0:DEPTH], at(1, 0)),
        halo(4, pack.at[1], from_behind.at[0, 1], at(1, 1)),
        halo(5, pack.at[1], from_ahead.at[0, 1], at(1, -1)),
    ]
    down = [
        halo(1, own.at[DEPTH:2 * DEPTH], own.at[last:last + DEPTH], at(-1, 0)),
        halo(6, pack.at[0], from_behind.at[2, 0], at(-1, 1)),
        halo(7, pack.at[0], from_ahead.at[2, 0], at(-1, -1)),
    ]
    across = [
        halo(2, pack, from_behind.at[1], at(0, 1)),
        halo(3, pack, from_ahead.at[1], at(0, -1)),
    ]
    for copy in across:
        copy.start()

    @pl.when(has_up)
    def _():
        for copy in up:
            copy.start()

    @pl.when(has_down)
    def _():
        for copy in down:
            copy.start()

    low = (lane % 8) < 4

    def unpack(dr, group, rows, shift):
        joined = jnp.where(low, from_ahead[dr, group], from_behind[dr, group])
        for r in rows:
            for f in range(4):
                index = (r % 4) * 4 + f
                side[shift + r, f] = joined if index == 0 else pltpu.roll(joined, 128 - 8 * index, axis=1)

    for copy in across:
        copy.wait_recv()
    unpack(1, 0, range(0, 4), DEPTH)
    unpack(1, 1, range(4, 8), DEPTH)

    @pl.when(has_down)
    def _():
        for copy in up:
            copy.wait_recv()
        unpack(0, 1, range(radii - DEPTH, radii), DEPTH - radii)

    @pl.when(jnp.logical_not(has_down))
    def _():
        own[0:DEPTH] = jnp.zeros((DEPTH, 4, 8, 128), jnp.float32)
        side[0:DEPTH] = jnp.zeros((DEPTH, 4, 8, 128), jnp.float32)

    def take_upper_halo():
        @pl.when(has_up)
        def _():
            for copy in down:
                copy.wait_recv()
            unpack(2, 0, range(0, DEPTH), last)

        @pl.when(jnp.logical_not(has_up))
        def _():
            own[last:last + DEPTH] = jnp.zeros((DEPTH, 4, 8, 128), jnp.float32)
            side[last:last + DEPTH] = jnp.zeros((DEPTH, 4, 8, 128), jnp.float32)

    def start_row(i):
        return jnp.concatenate([own[i, 0:3], side[i, 0:3]], axis=2)

    def row_facts(i):
        row = band * radii + i - DEPTH
        inside = jnp.logical_and(row >= 0, row < bands * radii)
        spin = rotation[jnp.clip(row, 0, bands * radii - 1)]
        return inside, spin, jnp.concatenate([own[i, 3], side[i, 3]], axis=1)

    def first_row(i, _):
        inside, spin, thick = row_facts(i)
        centre = start_row(i)
        rate = neighbour_rates(centre, start_row(i + 1), start_row(i - 1), thick, spin)
        first[i] = jnp.where(inside, centre + time_step * rate, 0.0)
        return 0

    def second_row(i, _):
        inside, spin, thick = row_facts(i)
        centre = first[i]
        rate = neighbour_rates(centre, first[i + 1], first[i - 1], thick, spin)
        second[i] = jnp.where(inside, 0.75 * start_row(i) + 0.25 * (centre + time_step * rate), 0.0)
        return 0

    starts = bounds_of(radii)

    def final_row(c, r):
        i = r + DEPTH
        inside, spin, thick = row_facts(i)
        centre = second[i]
        rate = neighbour_rates(centre, second[i + 1], second[i - 1], thick, spin)
        raws[c][place, r - starts[c]] = own[i, 0:3] / 3.0 + 2.0 / 3.0 * (centre + time_step * rate)[..., :128]

    def line_copy(to_right, d, c):
        held = raws[c].at[place]
        if to_right:
            return remote(held, held, right_sent.at[d, c], right_got.at[d, c], at(0, 2 * d))
        return remote(held, held, left_sent.at[d, c], left_got.at[d, c], at(0, -2 * d))

    def sends(to_right, d):
        return place + d <= places - 2 if to_right else place - d >= 1

    def gets(to_right, d):
        inner = jnp.logical_and(place >= 1, place <= places - 2)
        return jnp.logical_and(inner, place - d >= 0 if to_right else place + d <= places - 1)

    def send(c):
        for d in range(places - 2, 0, -1):
            for to_right in (True, False):
                @pl.when(sends(to_right, d))
                def _():
                    line_copy(to_right, d, c).start()

    def get(c):
        for d in range(1, places - 1):
            for to_right in (True, False):
                @pl.when(gets(to_right, d))
                def _():
                    line_copy(to_right, d, c).wait_recv()

    first_end, second_end = 1, 2
    for c in range(chunks):
        need_first = min(starts[c + 1] + DEPTH + 2, last + DEPTH - 1)
        need_second = min(starts[c + 1] + DEPTH + 1, last + DEPTH - 2)
        if first_end < last <= need_first:
            take_upper_halo()
        lax.fori_loop(first_end, need_first, first_row, 0, unroll=True)
        lax.fori_loop(second_end, need_second, second_row, 0, unroll=True)
        first_end, second_end = need_first, need_second
        for r in range(starts[c], starts[c + 1]):
            final_row(c, r)
        send(c)

    half = lax.broadcasted_iota(jnp.int32, (3, 8, 128), 2) < BLOCK
    total = 2 * sectors

    def sources(r, target):
        shift = shifts[0, band * radii + r]
        to_first = (2 * target - shift + total) % total // 2
        to_second = (2 * target + 1 - shift + total) % total // 2
        odd = shift % 2 == 1
        return jnp.where(odd, to_second, to_first), jnp.where(odd, to_first, to_second), odd

    def picked(c, r, target):
        low_from, high_from, _ = sources(r, target)
        return jnp.where(half, raws[c][low_from // 2, r - starts[c]], raws[c][high_from // 2, r - starts[c]])

    inner = jnp.logical_and(place >= 1, place <= places - 2)
    outer = jnp.logical_not(inner)
    beside = jnp.logical_or(place == 1, place == places - 2)
    mate = sector + 1 - 2 * parity
    end = sector + jnp.where(place == 1, -2, 2)
    end_mate = end + 1 - 2 * parity

    def mate_copy(c):
        return remote(staged[c].at[0], gots[c].at[parity], mate_sent.at[c], mate_got.at[c], (band, mate))

    def end_copy(other, c):
        target = lax.rem((end_mate if other else end) + sectors, sectors)
        return remote(
            staged[c].at[1 + other], gots[c].at[parity], end_sent.at[other, c], end_got.at[parity, c], (band, target)
        )

    def from_helper(q, c):
        return remote(gots[c].at[q], gots[c].at[q], end_sent.at[q, c], end_got.at[q, c], (band, mate))

    for c in range(chunks):
        get(c)
        rows = range(starts[c], starts[c + 1])

        @pl.when(beside)
        def _():
            for other, target in ((0, end), (1, end_mate)):
                for r in rows:
                    staged[c][1 + other, r - starts[c]] = picked(c, r, target)
                end_copy(other, c).start()

        @pl.when(inner)
        def _():
            for r in rows:
                staged[c][0, r - starts[c]] = picked(c, r, mate)
            mate_copy(c).start()
            for r in rows:
                gots[c][parity, r - starts[c]] = picked(c, r, sector)

    for c in range(chunks):
        @pl.when(inner)
        def _():
            mate_copy(c).wait_recv()

        @pl.when(outer)
        def _():
            for q in range(2):
                from_helper(q, c).wait_recv()

        for r in range(starts[c], starts[c + 1]):
            low_from, high_from, odd = sources(r, sector)
            moved = jnp.where(half, gots[c][low_from % 2, r - starts[c]], gots[c][high_from % 2, r - starts[c]])
            moved = jnp.where(odd, pltpu.roll(moved, BLOCK, axis=2), moved)
            for f in range(3):
                out[f, pl.ds(r, 8, stride=8), :] = moved[f]

    for copy in across:
        copy.wait_send()

    @pl.when(has_up)
    def _():
        for copy in up:
            copy.wait_send()

    @pl.when(has_down)
    def _():
        for copy in down:
            copy.wait_send()

    for c in range(chunks):
        @pl.when(beside)
        def _():
            for other in range(2):
                end_copy(other, c).wait_send()

        @pl.when(inner)
        def _():
            mate_copy(c).wait_send()

    for d in range(1, places - 1):
        for c in range(chunks):
            for to_right in (True, False):
                @pl.when(sends(to_right, d))
                def _():
                    line_copy(to_right, d, c).wait_send()


def body(fields, viscosity, rotation, shift_blocks):
    bands, sectors = lax.axis_size("rad"), lax.axis_size("azi")
    kinds, height, radii, width = fields.shape
    places = sectors // 2
    starts = bounds_of(radii)
    chunks = len(starts) - 1
    sizes = [starts[c + 1] - starts[c] for c in range(chunks)]
    rows = radii + 2 * DEPTH
    steps = places - 1
    vmem = lambda *shape: pltpu.VMEM(shape, jnp.float32)
    dma = lambda *shape: pltpu.SemaphoreType.DMA(shape)
    moved = pl.pallas_call(
        functools.partial(kernel, bands, sectors, chunks),
        out_shape=pltpu.VMEM((kinds, height * radii, width), jnp.float32),
        in_specs=[pl.BlockSpec(memory_space=pltpu.HBM)] * 4,
        out_specs=pl.BlockSpec(memory_space=pltpu.VMEM),
        scratch_shapes=[
            vmem(kinds, height * radii, width), vmem(radii, width),
            pltpu.SMEM(rotation.shape, jnp.float32), pltpu.SMEM(shift_blocks.shape, jnp.int32), dma(4),
            vmem(rows, 4, 8, 128), vmem(rows, 4, 8, 128),
            vmem(rows, 3, 8, 256), vmem(rows, 3, 8, 256),
            [vmem(places, size, 3, 8, 128) for size in sizes],
            [vmem(2, size, 3, 8, 128) for size in sizes],
            [vmem(3, size, 3, 8, 128) for size in sizes],
            vmem(2, 8, 128), vmem(3, 2, 8, 128), vmem(3, 2, 8, 128),
            dma(8), dma(8), dma(chunks), dma(chunks), dma(2, chunks), dma(2, chunks),
            dma(steps, chunks), dma(steps, chunks), dma(steps, chunks), dma(steps, chunks),
        ],
        compiler_params=pltpu.CompilerParams(collective_id=0, has_side_effects=True, vmem_limit_bytes=56 * 2**20),
        name="disc_step",
    )(fields.reshape(kinds, height * radii, width), viscosity, rotation, shift_blocks)
    return moved.reshape(fields.shape)


def solution(mesh):
    return jax.shard_map(
        body,
        mesh=mesh,
        in_specs=(P(None, None, "rad", "azi"), P("rad", "azi"), P(), P()),
        out_specs=P(None, None, "rad", "azi"),
        check_vma=False,
    )
```
